32 devices in a mesh: space: 8 (over z, y), tm: 4 (over x, core).
Axes of the slice: x: 2, y: 2, z: 4, core: 2. Of those that a mesh axis runs over, the one named last changes fastest.
Arguments:
- snapshots: bfloat16 [256, 65536], P('tm', 'space'), may hold values from -75 to 75
- prior_basis: bfloat16 [256, 65536], P('tm', 'space'), may hold values from -75 to 75
- mass_factor: bfloat16 [7, 64, 65536], P(None, None, 'space'), may hold values from -1 to 3.2, as said below
- neighbours: int32 [1024, 7], P('space'), may hold values from 0 to 1023, as said below
Outputs:
- merged_basis: bfloat16 [64, 65536], P(None, ('space', 'tm'))
- merged_weighted: bfloat16 [64, 65536], P(None, ('space', 'tm'))
The draws below stay inside these ranges and needn't reach their ends.
Inputs may be any that keep to these rules, and one draw needn't show every extreme that they name: `mass_factor`: factor entries; the diagonal of each block's own coupling lies in 1.5 to 3. neighbours[i, 0] = i; every entry lies within 8 blocks of i; in every draw some entries lie exactly 8 blocks below and above their block.
All inputs are finite; a program needn't handle non-finite values.
Results may differ from the reference program's by a relative error of at most 0.018.
Values may be sent and summed in bfloat16 or wider, within the bound.
No kernel may reach another device: no remote copies, remote signals or barrier semaphores. Data moves between devices by JAX's collectives and lax.ppermute only.
A program may use at most 128 MiB of HBM per device.

```python
import math
import jax
import jax.numpy as jnp
from jax import lax

BLOCK_DOFS = 64
RANK = 64
SNAPSHOTS = 64
NEIGHBOURS = 7
REACH = 8
SUBSPACE_STEPS = 3
LOCAL_BLOCKS = 128
BLOCKS = 1024
DOFS = 65536
TIME_SNAPSHOTS = 256
TIME_RANKS = 256
N_SPACE = 8
N_TM = 4


def scaled_rows(key, count, low, high):
    key_column, key_rough, key_entries = jax.random.split(key, 3)
    column_scale = jnp.exp(jax.random.uniform(key_column, (count, 1), jnp.float32, math.log(low), math.log(high)))
    position = jnp.arange(DOFS, dtype=jnp.float32) / DOFS
    roughness = jnp.exp(jax.random.uniform(key_rough, (1, DOFS), jnp.float32, math.log(0.5), math.log(2.0)))
    row_scale = jnp.power(3.0, position)[None, :] * roughness
    entries = jnp.clip(jax.random.normal(key_entries, (count, DOFS), jnp.float32), -4.0, 4.0)
    return entries * column_scale * row_scale


def draw_snapshots(key, part):
    return scaled_rows(jax.random.fold_in(key, 11), TIME_SNAPSHOTS, 0.3, 3.0).astype(jnp.bfloat16)


def draw_prior_basis(key, part):
    return scaled_rows(jax.random.fold_in(key, 23), TIME_RANKS, 0.3, 3.0).astype(jnp.bfloat16)


def draw_mass_factor(key, part):
    key_couple, key_diagonal = jax.random.split(jax.random.fold_in(key, 37), 2)
    spread = 1.0 / math.sqrt(BLOCK_DOFS * NEIGHBOURS)
    couples = jnp.clip(jax.random.normal(key_couple, (NEIGHBOURS, BLOCK_DOFS, DOFS), jnp.float32), -4.0, 4.0) * spread
    diagonal_values = jnp.exp(jax.random.uniform(key_diagonal, (DOFS,), jnp.float32, math.log(1.5), math.log(3.0)))
    row_place = jnp.arange(DOFS) % BLOCK_DOFS
    column_place = jnp.arange(BLOCK_DOFS)
    slot_index = jnp.arange(NEIGHBOURS)
    on_diagonal = (slot_index[:, None, None] == 0) & (column_place[None, :, None] == row_place[None, None, :])
    return jnp.where(on_diagonal, diagonal_values[None, None, :], couples).astype(jnp.bfloat16)


def draw_neighbours(key, part):
    offsets = jax.random.randint(jax.random.fold_in(key, 41), (BLOCKS, NEIGHBOURS), -REACH, REACH + 1)
    block_index = jnp.arange(BLOCKS, dtype=jnp.int32)[:, None]
    slot_index = jnp.arange(NEIGHBOURS, dtype=jnp.int32)[None, :]
    offsets = jnp.where(slot_index == 0, 0, offsets)
    position = block_index % LOCAL_BLOCKS
    offsets = jnp.where((slot_index == 1) & (position == 0), -REACH, offsets)
    offsets = jnp.where((slot_index == 1) & (position == LOCAL_BLOCKS - 1), REACH, offsets)
    return jnp.clip(block_index + offsets, 0, BLOCKS - 1).astype(jnp.int32)


def setup_inputs(seed: int = 0) -> dict:
    streams_of = jax.random.split(jax.random.key(seed), 5)
    snapshots = draw_snapshots(jax.random.fold_in(streams_of[4], 71), 0)
    prior_basis = draw_prior_basis(jax.random.fold_in(streams_of[4], 71), 0)
    mass_factor = draw_mass_factor(jax.random.fold_in(streams_of[4], 71), 0)
    neighbours = draw_neighbours(jax.random.fold_in(streams_of[4], 71), 0)
    return {"snapshots": snapshots, "prior_basis": prior_basis, "mass_factor": mass_factor, "neighbours": neighbours}


def weigh_rows(stacked, mass_factor, neighbours):
    columns = stacked.shape[0]
    blocks = stacked.reshape(columns, BLOCKS, BLOCK_DOFS)

    def one_slab(slab_index):
        first_row = slab_index * LOCAL_BLOCKS
        slab_rows = lax.dynamic_slice_in_dim(neighbours, first_row, LOCAL_BLOCKS, 0)
        picked = jnp.take(blocks, slab_rows, axis=1).astype(jnp.float32)
        factor = lax.dynamic_slice_in_dim(mass_factor, first_row * BLOCK_DOFS, LOCAL_BLOCKS * BLOCK_DOFS, 2)
        factor = factor.reshape(NEIGHBOURS, BLOCK_DOFS, LOCAL_BLOCKS, BLOCK_DOFS).astype(jnp.float32)
        return jnp.einsum('cbkq,kqbr->cbr', picked, factor).astype(jnp.bfloat16)
    slabs = lax.map(one_slab, jnp.arange(N_SPACE, dtype=jnp.int32))
    return jnp.transpose(slabs, (1, 0, 2, 3)).reshape(columns, DOFS)

def compress(gram_total):
    highest = lax.Precision.HIGHEST
    order_size = gram_total.shape[0]
    weights = jnp.eye(order_size, RANK, dtype=jnp.float32)
    for repeat in range(SUBSPACE_STEPS):
        product = jnp.dot(gram_total, weights, precision=highest)
        inner_gram = jnp.dot(product.T, jnp.dot(gram_total, product, precision=highest), precision=highest)
        scales = jnp.sqrt(jnp.diagonal(inner_gram))
        factor_lower = jnp.linalg.cholesky(inner_gram / (scales[:, None] * scales[None, :]))
        normed = product / scales[None, :]
        weights = lax.linalg.triangular_solve(factor_lower, normed, left_side=False, lower=True, transpose_a=True)
    product = jnp.dot(gram_total, weights, precision=highest)
    lengths = jnp.sqrt(lax.optimization_barrier(jnp.sum(product * product, axis=0)) + 1e-06)
    return (weights * lengths[None, :]).astype(jnp.bfloat16)

def reduce_pair(stacked, weighted):
    gram_total = jnp.dot(weighted.astype(jnp.float32), weighted.T.astype(jnp.float32), preferred_element_type=jnp.float32)
    coefficients = compress(gram_total)
    basis = jnp.dot(coefficients.T.astype(jnp.float32), stacked.astype(jnp.float32), preferred_element_type=jnp.float32).astype(jnp.bfloat16)
    weighted_basis = jnp.dot(coefficients.T.astype(jnp.float32), weighted.astype(jnp.float32), preferred_element_type=jnp.float32).astype(jnp.bfloat16)
    return (basis, weighted_basis)

def reference(snapshots, prior_basis, mass_factor, neighbours):
    groups = []
    for member in range(N_TM):
        stacked = jnp.concatenate([prior_basis[member * RANK:(member + 1) * RANK], snapshots[member * SNAPSHOTS:(member + 1) * SNAPSHOTS]], axis=0)
        groups.append(reduce_pair(stacked, weigh_rows(stacked, mass_factor, neighbours)))
    stride = 1
    while stride < N_TM:
        merged = list(groups)
        for member in range(N_TM):
            if member % (2 * stride) < stride:
                lower_pair = groups[member]
                upper_pair = groups[member + stride]
                stacked = jnp.concatenate([lower_pair[0], upper_pair[0]], axis=0)
                weighted = jnp.concatenate([lower_pair[1], upper_pair[1]], axis=0)
                result = reduce_pair(stacked, weighted)
                merged[member] = result
                merged[member + stride] = result
        groups = merged
        stride = stride * 2
    return (groups[0][0], groups[0][1])
```

```python
import functools
import jax
import jax.numpy as jnp
from jax import lax
from jax.experimental import pallas as pl
from jax.experimental.pallas import tpu as pltpu
from jax.sharding import PartitionSpec as P

BLOCK_DOFS = 64
RANK = 64
REACH = 8
SUBSPACE_STEPS = 3
PANEL = 8
TILE = 128
F32 = jnp.float32
BF16 = jnp.bfloat16
HIGHEST = lax.Precision.HIGHEST
NT = (((1,), (1,)), ((), ()))


def halo(block, axis, width):
    count = lax.axis_size(axis)
    forward = [(i, i + 1) for i in range(count - 1)]
    backward = [(target, source) for source, target in forward]
    low = lax.ppermute(block[:, block.shape[1] - width:], axis, forward)
    high = lax.ppermute(block[:, :width], axis, backward)
    return low, high


def total(block, axis):
    count = lax.axis_size(axis)
    if count & (count - 1):
        return lax.psum(block, axis)
    step = 1
    while step < count:
        block = block + lax.ppermute(block, axis, [(i, i ^ step) for i in range(count)])
        step *= 2
    return block


def partner(block, axis, bit):
    count = lax.axis_size(axis)
    route = []
    for low in range(count):
        high = low | 1 << bit
        if high != low and high < count:
            route += [(low, high), (high, low)]
    return lax.ppermute(block, axis, route)


def weigh_kernel(spots, prior_ref, snap_ref, low_ref, high_ref, factor_ref, weighted_ref, gram_ref, bank):
    step = pl.program_id(0)
    rows, width = prior_ref.shape
    edge = low_ref.shape[1]
    neighbours, block, chunk = factor_ref.shape
    columns = bank.shape[0]
    whole = width + 2 * edge

    @pl.when(step == 0)
    def _():
        bank[:, 0:edge] = low_ref[...]
        bank[:rows, edge:edge + width] = prior_ref[...]
        bank[rows:, edge:edge + width] = snap_ref[...]
        bank[:, edge + width:whole] = high_ref[...]
        bank[:, whole + TILE:2 * whole] = bank[:, block:whole - block]
        bank[:, whole:whole + TILE] = bank[:, 0:TILE]
        bank[:, whole + block:whole + TILE] = bank[:, 0:block]
        bank[:, 2 * whole:2 * whole + TILE] = bank[:, whole - TILE:whole]
        bank[:, 2 * whole:2 * whole + block] = bank[:, whole - block:whole]
        gram_ref[...] = jnp.zeros_like(gram_ref)

    lower = lax.broadcasted_iota(jnp.int32, (columns, TILE), 1) < block
    pieces = []
    for tile in range(chunk // TILE):
        results = []
        for side in range(2):
            row = step * (chunk // block) + tile * 2 + side
            parts = []
            for k in range(neighbours):
                spot = spots[row * neighbours + k]
                parts.append(bank[:, pl.ds(pl.multiple_of(spot * TILE, TILE), TILE)])
            joined = [jnp.where(lower, parts[k], parts[k + 1]) for k in range(0, neighbours - 1, 2)]
            if neighbours % 2:
                joined.append(parts[-1][:, :block])
            results.append(jnp.concatenate(joined, axis=1))
        left = jnp.concatenate(results, axis=0)
        right = factor_ref[:, :, tile * TILE:(tile + 1) * TILE].reshape(neighbours * block, TILE)
        product = jnp.dot(left, right, preferred_element_type=F32)
        pieces.append(jnp.where(lower, product[:columns], product[columns:]).astype(BF16))
    weighted = jnp.concatenate(pieces, axis=1)
    weighted_ref[...] = weighted
    gram_ref[...] += lax.dot_general(weighted, weighted, NT, preferred_element_type=F32)


def weigh(prior, snapshots, low, high, factor, neighbours):
    rows, width = prior.shape
    columns = 2 * rows
    count, block, _ = factor.shape
    edge = low.shape[1]
    whole = width + 2 * edge
    local = neighbours - (lax.axis_index("space") * (width // block) - edge // block)
    half, odd = local // 2, local % 2
    side = jnp.arange(count, dtype=jnp.int32)[None, :] % 2
    spots = half + jnp.where(side == 0, odd * (whole // TILE + 1), (1 - odd) * (whole // TILE))
    chunk = min(width, 1024)
    full = lambda i, s: (0, 0)
    return pl.pallas_call(
        weigh_kernel,
        out_shape=(
            jax.ShapeDtypeStruct((columns, width), BF16),
            jax.ShapeDtypeStruct((columns, columns), F32),
        ),
        grid_spec=pltpu.PrefetchScalarGridSpec(
            num_scalar_prefetch=1,
            grid=(width // chunk,),
            in_specs=[
                pl.BlockSpec((rows, width), full),
                pl.BlockSpec((rows, width), full),
                pl.BlockSpec((columns, edge), full),
                pl.BlockSpec((columns, edge), full),
                pl.BlockSpec((count, block, chunk), lambda i, s: (0, 0, i)),
            ],
            out_specs=(
                pl.BlockSpec((columns, chunk), lambda i, s: (0, i)),
                pl.BlockSpec((columns, columns), full),
            ),
            scratch_shapes=[pltpu.VMEM((columns, 2 * whole + TILE), BF16)],
        ),
        compiler_params=pltpu.CompilerParams(vmem_limit_bytes=40 * 1024 * 1024),
        name="weigh",
    )(spots.reshape(-1).astype(jnp.int32), prior, snapshots, low, high, factor)


def lanes_of(group, column):
    return jnp.broadcast_to(group[:, column:column + 1], (group.shape[0], TILE))


def row_of(group, row):
    return jnp.broadcast_to(group[row:row + 1, :], group.shape)


def eliminate(left, right, solved):
    groups = left.shape[0]
    sub = lax.broadcasted_iota(jnp.int32, (PANEL, TILE), 0)

    def panel(p, _):
        pivot, image = left[p], right[p]
        cols = [lanes_of(pivot, s) for s in range(PANEL)]
        d = [[row_of(cols[c], r) if r >= c else None for c in range(PANEL)] for r in range(PANEL)]
        rows_a = [row_of(pivot, r) for r in range(PANEL)]
        rows_n = [row_of(image, r) for r in range(PANEL)]
        inverse = []
        for s in range(PANEL):
            inverse.append(1.0 / d[s][s])
            for r in range(s + 1, PANEL):
                m = d[r][s] * inverse[s]
                for c in range(s + 1, r + 1):
                    d[r][c] = d[r][c] - m * d[c][s]
                rows_a[r] = rows_a[r] - m * rows_a[s]
                rows_n[r] = rows_n[r] - m * rows_n[s]
        for q in range(groups):
            fresh_a, fresh_n = left[q], right[q]
            work = [lanes_of(fresh_a, s) for s in range(PANEL)]
            for s in range(PANEL):
                factor = work[s] * inverse[s]
                for c in range(s + 1, PANEL):
                    work[c] = work[c] - factor * d[c][s]
                fresh_a = fresh_a - factor * rows_a[s]
                fresh_n = fresh_n - factor * rows_n[s]
            left[q] = pltpu.roll(fresh_a, TILE - PANEL, 1)
            right[q] = fresh_n
        merged = rows_n[0] * lax.rsqrt(d[0][0])
        for r in range(1, PANEL):
            merged = jnp.where(sub == r, rows_n[r] * lax.rsqrt(d[r][r]), merged)
        solved[p] = merged
        return 0

    lax.fori_loop(0, groups, panel, 0)


def compress_kernel(gram_ref, out_ref, left, right, solved):
    gram = gram_ref[...]

    product = gram[:RANK]
    for _ in range(SUBSPACE_STEPS):
        image = jnp.dot(product, gram, precision=HIGHEST, preferred_element_type=F32)
        scale = 1.0 / jnp.sqrt(jnp.sum(product * image, axis=1, keepdims=True))
        normed = product * scale
        image = jnp.concatenate([image * scale, jnp.zeros((TILE - RANK, TILE), F32)], axis=0)
        inner = lax.dot_general(normed, image, NT, precision=HIGHEST, preferred_element_type=F32)
        left[...] = inner.reshape(left.shape)
        right[...] = normed.reshape(right.shape)
        eliminate(left, right, solved)
        weights = solved[...].reshape(RANK, TILE)
        product = jnp.dot(weights, gram, precision=HIGHEST, preferred_element_type=F32)
    lengths = jnp.sqrt(jnp.sum(product * product, axis=1, keepdims=True) + 1e-06)
    out_ref[...] = (solved[...].reshape(RANK, TILE) * lengths).astype(BF16)


def compress(gram):
    order = gram.shape[0]
    return pl.pallas_call(
        compress_kernel,
        out_shape=jax.ShapeDtypeStruct((RANK, order), BF16),
        scratch_shapes=[pltpu.VMEM((RANK // PANEL, PANEL, TILE), F32)] * 3,
        compiler_params=pltpu.CompilerParams(vmem_limit_bytes=16 * 1024 * 1024),
        name="compress",
    )(gram)


def combine(coefficients, rows):
    return jnp.dot(coefficients, rows, preferred_element_type=F32).astype(BF16)


def ordered(upper_half, own_rows, partner_rows):
    lower_part = jnp.where(upper_half, partner_rows, own_rows)
    upper_part = jnp.where(upper_half, own_rows, partner_rows)
    return jnp.concatenate([lower_part, upper_part], axis=0)


def shards(snapshots, prior_basis, mass_factor, neighbours):
    stacked = jnp.concatenate([prior_basis, snapshots], axis=0)
    low, high = halo(stacked, "space", REACH * BLOCK_DOFS)
    weighted, gram = weigh(prior_basis, snapshots, low, high, mass_factor, neighbours)
    coefficients = compress(total(gram, "space"))
    basis, weighted_basis = combine(coefficients, stacked), combine(coefficients, weighted)
    member = lax.axis_index("tm")
    for level_bit in range(lax.axis_size("tm").bit_length() - 1):
        upper_half = member // (1 << level_bit) % 2 == 1
        weighted = ordered(upper_half, weighted_basis, partner(weighted_basis, "tm", level_bit))
        stacked = ordered(upper_half, basis, partner(basis, "tm", level_bit))
        gram = lax.dot_general(weighted, weighted, NT, preferred_element_type=F32)
        coefficients = compress(total(gram, "space"))
        basis, weighted_basis = combine(coefficients, stacked), combine(coefficients, weighted)
    share_width = basis.shape[1] // lax.axis_size("tm")
    basis_share = lax.dynamic_slice_in_dim(basis, member * share_width, share_width, 1)
    weighted_share = lax.dynamic_slice_in_dim(weighted_basis, member * share_width, share_width, 1)
    return (basis_share, weighted_share)


def solution(mesh):
    return jax.shard_map(
        shards,
        mesh=mesh,
        in_specs=(P("tm", "space"), P("tm", "space"), P(None, None, "space"), P("space", None)),
        out_specs=(P(None, ("space", "tm")), P(None, ("space", "tm"))),
        check_vma=False,
    )
```

```python
import functools
import jax
import jax.numpy as jnp
from jax import lax
from jax.experimental import pallas as pl
from jax.experimental.pallas import tpu as pltpu
from jax.sharding import PartitionSpec as P

BLOCK_DOFS = 64
RANK = 64
REACH = 8
SUBSPACE_STEPS = 3
PANEL = 8
TILE = 128
F32 = jnp.float32
BF16 = jnp.bfloat16
HIGHEST = lax.Precision.HIGHEST
NT = (((1,), (1,)), ((), ()))


def halo(block, axis, width):
    count = lax.axis_size(axis)
    forward = [(i, i + 1) for i in range(count - 1)]
    backward = [(target, source) for source, target in forward]
    low = lax.ppermute(block[:, block.shape[1] - width:], axis, forward)
    high = lax.ppermute(block[:, :width], axis, backward)
    return low, high


def swapped(block, axis, step):
    return lax.ppermute(block, axis, [(i, i ^ step) for i in range(lax.axis_size(axis))])


def total(block, axis, limit=None):
    count = limit or lax.axis_size(axis)
    step = 1
    while step < count:
        block = block + swapped(block, axis, step)
        step *= 2
    return block


def weigh_kernel(spots, prior_ref, snap_ref, low_ref, high_ref, factor_ref, weighted_ref, gram_ref, bank):
    step = pl.program_id(0)
    rows, width = prior_ref.shape
    edge = low_ref.shape[1]
    neighbours, block, chunk = factor_ref.shape
    columns = bank.shape[0]
    whole = width + 2 * edge

    @pl.when(step == 0)
    def _():
        bank[:, 0:edge] = low_ref[...]
        bank[:rows, edge:edge + width] = prior_ref[...]
        bank[rows:, edge:edge + width] = snap_ref[...]
        bank[:, edge + width:whole] = high_ref[...]
        bank[:, whole + TILE:2 * whole] = bank[:, block:whole - block]
        bank[:, whole:whole + TILE] = bank[:, 0:TILE]
        bank[:, whole + block:whole + TILE] = bank[:, 0:block]
        bank[:, 2 * whole:2 * whole + TILE] = bank[:, whole - TILE:whole]
        bank[:, 2 * whole:2 * whole + block] = bank[:, whole - block:whole]
        gram_ref[...] = jnp.zeros_like(gram_ref)

    lower = lax.broadcasted_iota(jnp.int32, (columns, TILE), 1) < block
    pieces = []
    for tile in range(chunk // TILE):
        results = []
        for side in range(2):
            row = step * (chunk // block) + tile * 2 + side
            parts = []
            for k in range(neighbours):
                spot = spots[row * neighbours + k]
                parts.append(bank[:, pl.ds(pl.multiple_of(spot * TILE, TILE), TILE)])
            joined = [jnp.where(lower, parts[k], parts[k + 1]) for k in range(0, neighbours - 1, 2)]
            if neighbours % 2:
                joined.append(parts[-1][:, :block])
            results.append(jnp.concatenate(joined, axis=1))
        left = jnp.concatenate(results, axis=0)
        right = factor_ref[:, :, tile * TILE:(tile + 1) * TILE].reshape(neighbours * block, TILE)
        product = jnp.dot(left, right, preferred_element_type=F32)
        pieces.append(jnp.where(lower, product[:columns], product[columns:]).astype(BF16))
    weighted = jnp.concatenate(pieces, axis=1)
    weighted_ref[...] = weighted
    gram_ref[...] += lax.dot_general(weighted, weighted, NT, preferred_element_type=F32)


def weigh(prior, snapshots, low, high, factor, neighbours):
    rows, width = prior.shape
    columns = 2 * rows
    count, block, _ = factor.shape
    edge = low.shape[1]
    whole = width + 2 * edge
    local = neighbours - (lax.axis_index("space") * (width // block) - edge // block)
    half, odd = local // 2, local % 2
    side = jnp.arange(count, dtype=jnp.int32)[None, :] % 2
    spots = half + jnp.where(side == 0, odd * (whole // TILE + 1), (1 - odd) * (whole // TILE))
    chunk = min(width, 1024)
    full = lambda i, s: (0, 0)
    return pl.pallas_call(
        weigh_kernel,
        out_shape=(
            jax.ShapeDtypeStruct((columns, width), BF16),
            jax.ShapeDtypeStruct((columns, columns), F32),
        ),
        grid_spec=pltpu.PrefetchScalarGridSpec(
            num_scalar_prefetch=1,
            grid=(width // chunk,),
            in_specs=[
                pl.BlockSpec((rows, width), full),
                pl.BlockSpec((rows, width), full),
                pl.BlockSpec((columns, edge), full),
                pl.BlockSpec((columns, edge), full),
                pl.BlockSpec((count, block, chunk), lambda i, s: (0, 0, i)),
            ],
            out_specs=(
                pl.BlockSpec((columns, chunk), lambda i, s: (0, i)),
                pl.BlockSpec((columns, columns), full),
            ),
            scratch_shapes=[pltpu.VMEM((columns, 2 * whole + TILE), BF16)],
        ),
        compiler_params=pltpu.CompilerParams(vmem_limit_bytes=40 * 1024 * 1024),
        name="weigh",
    )(spots.reshape(-1).astype(jnp.int32), prior, snapshots, low, high, factor)


def lanes_of(group, column):
    return jnp.broadcast_to(group[:, column:column + 1], (group.shape[0], TILE))


def row_of(group, row):
    return jnp.broadcast_to(group[row:row + 1, :], group.shape)


def eliminate(left, right, solved):
    groups = left.shape[0]
    sub = lax.broadcasted_iota(jnp.int32, (PANEL, TILE), 0)

    def panel(p, _):
        pivot, image = left[p], right[p]
        cols = [lanes_of(pivot, s) for s in range(PANEL)]
        d = [[row_of(cols[c], r) if r >= c else None for c in range(PANEL)] for r in range(PANEL)]
        rows_a = [row_of(pivot, r) for r in range(PANEL)]
        rows_n = [row_of(image, r) for r in range(PANEL)]
        inverse = []
        for s in range(PANEL):
            inverse.append(1.0 / d[s][s])
            for r in range(s + 1, PANEL):
                m = d[r][s] * inverse[s]
                for c in range(s + 1, r + 1):
                    d[r][c] = d[r][c] - m * d[c][s]
                rows_a[r] = rows_a[r] - m * rows_a[s]
                rows_n[r] = rows_n[r] - m * rows_n[s]
        for q in range(groups):
            fresh_a, fresh_n = left[q], right[q]
            work = [lanes_of(fresh_a, s) for s in range(PANEL)]
            for s in range(PANEL):
                factor = work[s] * inverse[s]
                for c in range(s + 1, PANEL):
                    work[c] = work[c] - factor * d[c][s]
                fresh_a = fresh_a - factor * rows_a[s]
                fresh_n = fresh_n - factor * rows_n[s]
            left[q] = pltpu.roll(fresh_a, TILE - PANEL, 1)
            right[q] = fresh_n
        merged = rows_n[0] * lax.rsqrt(d[0][0])
        for r in range(1, PANEL):
            merged = jnp.where(sub == r, rows_n[r] * lax.rsqrt(d[r][r]), merged)
        solved[p] = merged
        return 0

    lax.fori_loop(0, groups, panel, 0)


def reduce_gram(gram, left, right, solved):
    product = gram[:RANK]
    for _ in range(SUBSPACE_STEPS):
        image = jnp.dot(product, gram, precision=HIGHEST, preferred_element_type=F32)
        scale = 1.0 / jnp.sqrt(jnp.sum(product * image, axis=1, keepdims=True))
        normed = product * scale
        image = jnp.concatenate([image * scale, jnp.zeros((TILE - RANK, TILE), F32)], axis=0)
        inner = lax.dot_general(normed, image, NT, precision=HIGHEST, preferred_element_type=F32)
        left[...] = inner.reshape(left.shape)
        right[...] = normed.reshape(right.shape)
        eliminate(left, right, solved)
        weights = solved[...].reshape(RANK, TILE)
        product = jnp.dot(weights, gram, precision=HIGHEST, preferred_element_type=F32)
    lengths = jnp.sqrt(jnp.sum(product * product, axis=1, keepdims=True) + 1e-06)
    return (solved[...].reshape(RANK, TILE) * lengths).astype(BF16)


def inner_of(coefficients, gram):
    wide = coefficients.astype(F32)
    image = jnp.dot(wide, gram, precision=HIGHEST, preferred_element_type=F32)
    return lax.dot_general(image, wide, NT, precision=HIGHEST, preferred_element_type=F32)


def first_kernel(gram_ref, out_ref, own_ref, left, right, solved):
    gram = gram_ref[...]
    coefficients = reduce_gram(gram, left, right, solved)
    out_ref[...] = coefficients
    own_ref[...] = inner_of(coefficients, gram)


def merge_kernel(top_ref, upper_ref, out_ref, own_ref, left, right, solved):
    top = top_ref[...]
    bottom = jnp.concatenate([top.T[RANK:], upper_ref[...]], axis=1)
    gram = jnp.concatenate([top, bottom], axis=0)
    coefficients = reduce_gram(gram, left, right, solved)
    out_ref[...] = coefficients
    own_ref[...] = inner_of(coefficients, gram)


def compress(kernel, *gram):
    return pl.pallas_call(
        kernel,
        out_shape=(
            jax.ShapeDtypeStruct((RANK, gram[0].shape[1]), BF16),
            jax.ShapeDtypeStruct((RANK, RANK), F32),
        ),
        scratch_shapes=[pltpu.VMEM((RANK // PANEL, PANEL, TILE), F32)] * 3,
        compiler_params=pltpu.CompilerParams(vmem_limit_bytes=16 * 1024 * 1024),
        name="compress",
    )(*gram)


def combine(coefficients, rows):
    return jnp.dot(coefficients, rows, preferred_element_type=F32).astype(BF16)


def shared_out(rows, width, bit):
    pieces = [
        lax.dynamic_slice_in_dim(rows, (2 * pair + bit) * width, width, 1)
        for pair in range(rows.shape[1] // (2 * width))
    ]
    return pieces[0] if len(pieces) == 1 else jnp.concatenate(pieces, axis=1)


def ordered(upper_half, own_rows, partner_rows):
    lower_part = jnp.where(upper_half, partner_rows, own_rows)
    upper_part = jnp.where(upper_half, own_rows, partner_rows)
    return jnp.concatenate([lower_part, upper_part], axis=0)


def shards(snapshots, prior_basis, mass_factor, neighbours):
    stacked = jnp.concatenate([prior_basis, snapshots], axis=0)
    low, high = halo(stacked, "space", REACH * BLOCK_DOFS)
    weighted, gram = weigh(prior_basis, snapshots, low, high, mass_factor, neighbours)
    coefficients, own = compress(first_kernel, total(gram, "space"))
    members = lax.axis_size("tm")
    member = lax.axis_index("tm")
    width = stacked.shape[1] // members
    for level in range(members.bit_length() - 1):
        step = 1 << level
        bit = member // step % 2
        upper_half = bit == 1
        weighted = combine(coefficients, weighted)
        sent = swapped(shared_out(weighted, width, 1 - bit), "tm", step)
        partner_own = swapped(own, "tm", step)
        weighted = ordered(upper_half, shared_out(weighted, width, bit), sent)
        stacked = combine(coefficients, stacked)
        sent = swapped(shared_out(stacked, width, 1 - bit), "tm", step)
        stacked = ordered(upper_half, shared_out(stacked, width, bit), sent)
        top = lax.dot_general(weighted[:RANK], weighted, NT, preferred_element_type=F32)
        top = total(total(top, "tm", 2 * step), "space")
        coefficients, own = compress(merge_kernel, top, jnp.where(upper_half, own, partner_own))
    return combine(coefficients, stacked), combine(coefficients, weighted)


def solution(mesh):
    return jax.shard_map(
        shards,
        mesh=mesh,
        in_specs=(P("tm", "space"), P("tm", "space"), P(None, None, "space"), P("space", None)),
        out_specs=(P(None, ("space", "tm")), P(None, ("space", "tm"))),
        check_vma=False,
    )
```

```python
import functools
import jax
import jax.numpy as jnp
from jax import lax
from jax.experimental import pallas as pl
from jax.experimental.pallas import tpu as pltpu
from jax.sharding import PartitionSpec as P

BLOCK_DOFS = 64
RANK = 64
REACH = 8
SUBSPACE_STEPS = 3
PANEL = 8
TILE = 128
F32 = jnp.float32
BF16 = jnp.bfloat16
HIGHEST = lax.Precision.HIGHEST
NT = (((1,), (1,)), ((), ()))


def halo(block, axis, width):
    count = lax.axis_size(axis)
    forward = [(i, i + 1) for i in range(count - 1)]
    backward = [(target, source) for source, target in forward]
    low = lax.ppermute(block[:, block.shape[1] - width:], axis, forward)
    high = lax.ppermute(block[:, :width], axis, backward)
    return low, high


def swapped(block, mask):
    axes = ("space", "tm")
    count = lax.axis_size("space") * lax.axis_size("tm")
    return lax.ppermute(block, axes, [(i, i ^ mask) for i in range(count)])


def total(block, bits):
    for start in range(0, len(bits), 2):
        first = bits[start]
        if start + 1 < len(bits):
            second = bits[start + 1]
            near, far, both = swapped(block, first), swapped(block, second), swapped(block, first | second)
            block = (block + near) + (far + both)
        else:
            block = block + swapped(block, first)
    return block


def fill_odd(bank, whole, block, start, stop):
    bank[:, whole + start + TILE:whole + stop] = bank[:, start + block:stop - block]


def weigh_chunk(spots, row, bank, factor_ref):
    neighbours, block, chunk = factor_ref.shape
    columns = bank.shape[0]
    lower = lax.broadcasted_iota(jnp.int32, (columns, TILE), 1) < block
    pieces = []
    for tile in range(chunk // TILE):
        results = []
        for side in range(2):
            parts = []
            for k in range(neighbours):
                spot = spots[(row + tile * 2 + side) * neighbours + k]
                parts.append(bank[:, pl.ds(pl.multiple_of(spot * TILE, TILE), TILE)])
            joined = [jnp.where(lower, parts[k], parts[k + 1]) for k in range(0, neighbours - 1, 2)]
            if neighbours % 2:
                joined.append(parts[-1][:, :block])
            results.append(jnp.concatenate(joined, axis=1))
        left = jnp.concatenate(results, axis=0)
        right = factor_ref[:, :, tile * TILE:(tile + 1) * TILE].reshape(neighbours * block, TILE)
        product = jnp.dot(left, right, preferred_element_type=F32)
        pieces.append(jnp.where(lower, product[:columns], product[columns:]).astype(BF16))
    return jnp.concatenate(pieces, axis=1)


def inside_kernel(edge, spots, prior_ref, snap_ref, factor_ref, weighted_ref, gram_ref, bank):
    step = pl.program_id(0)
    rows, width = prior_ref.shape
    _, block, chunk = factor_ref.shape
    whole = width + 2 * edge

    @pl.when(step == 0)
    def _():
        bank[:rows, edge:edge + width] = prior_ref[...]
        bank[rows:, edge:edge + width] = snap_ref[...]
        fill_odd(bank, whole, block, edge, edge + width)
        gram_ref[...] = jnp.zeros_like(gram_ref)

    weighted = weigh_chunk(spots, (step + 1) * (chunk // block), bank, factor_ref)
    weighted_ref[...] = weighted
    gram_ref[...] += lax.dot_general(weighted, weighted, NT, preferred_element_type=F32)


def border_kernel(
    spots, prior_ref, snap_ref, low_ref, high_ref, factor_ref, part_ref, kept_ref, weighted_ref, gram_ref, bank
):
    step = pl.program_id(0)
    rows, span = prior_ref.shape
    edge = low_ref.shape[1]
    _, block, chunk = factor_ref.shape
    whole = span + edge

    @pl.when(step == 0)
    def _():
        bank[:, :edge] = low_ref[...]
        bank[:rows, edge:whole] = prior_ref[...]
        bank[rows:, edge:whole] = snap_ref[...]
        gram_ref[...] = part_ref[...]

    @pl.when(step != 0)
    def _():
        bank[:rows, :span] = prior_ref[...]
        bank[rows:, :span] = snap_ref[...]
        bank[:, span:whole] = high_ref[...]

    fill_odd(bank, whole, block, 0, whole)
    bank[:, whole + block:whole + TILE] = bank[:, :block]
    bank[:, 2 * whole:2 * whole + block] = bank[:, whole - block:whole]
    weighted = weigh_chunk(spots, step * (chunk // block), bank, factor_ref)
    weighted_ref[...] = weighted
    gram_ref[...] += lax.dot_general(weighted, weighted, NT, preferred_element_type=F32)


def spots_of(local, tiles):
    half, odd = local // 2, local % 2
    side = jnp.arange(local.shape[1], dtype=jnp.int32)[None, :] % 2
    spots = half + jnp.where(side == 0, odd * (tiles + 1), (1 - odd) * tiles)
    return spots.reshape(-1).astype(jnp.int32)


def weigh(prior, snapshots, factor, neighbours):
    rows, width = prior.shape
    columns = 2 * rows
    count, block, _ = factor.shape
    edge = REACH * block
    chunk = 2 * edge
    span = 2 * chunk
    chunks = width // chunk
    low, high = halo(jnp.concatenate([prior, snapshots], axis=0), "space", edge)
    local = neighbours - (lax.axis_index("space") * (width // block) - REACH)
    per = chunk // block
    shift = (width - span + edge) // block
    near = jnp.concatenate([local[:per], local[-per:] - shift], axis=0)
    full = lambda i, s: (0, 0)
    shapes = (
        jax.ShapeDtypeStruct((columns, width), BF16),
        jax.ShapeDtypeStruct((columns, columns), F32),
    )
    params = pltpu.CompilerParams(vmem_limit_bytes=56 * 1024 * 1024)
    weighted, gram = pl.pallas_call(
        functools.partial(inside_kernel, edge),
        out_shape=shapes,
        grid_spec=pltpu.PrefetchScalarGridSpec(
            num_scalar_prefetch=1,
            grid=(chunks - 2,),
            in_specs=[
                pl.BlockSpec((rows, width), full),
                pl.BlockSpec((rows, width), full),
                pl.BlockSpec((count, block, chunk), lambda i, s: (0, 0, i + 1)),
            ],
            out_specs=(
                pl.BlockSpec((columns, chunk), lambda i, s: (0, i + 1)),
                pl.BlockSpec((columns, columns), full),
            ),
            scratch_shapes=[pltpu.VMEM((columns, 2 * (width + 2 * edge) + TILE), BF16)],
        ),
        compiler_params=params,
        cost_estimate=pl.CostEstimate(
            flops=8 * columns * count * block * width, bytes_accessed=2 * factor.size, transcendentals=0
        ),
        name="weigh_inside",
    )(spots_of(local, (width + 2 * edge) // TILE), prior, snapshots, factor)
    ends = width // span - 1
    return pl.pallas_call(
        border_kernel,
        out_shape=shapes,
        grid_spec=pltpu.PrefetchScalarGridSpec(
            num_scalar_prefetch=1,
            grid=(2,),
            in_specs=[
                pl.BlockSpec((rows, span), lambda i, s: (0, i * ends)),
                pl.BlockSpec((rows, span), lambda i, s: (0, i * ends)),
                pl.BlockSpec((columns, edge), full),
                pl.BlockSpec((columns, edge), full),
                pl.BlockSpec((count, block, chunk), lambda i, s: (0, 0, i * (chunks - 1))),
                pl.BlockSpec((columns, columns), full),
                pl.BlockSpec(memory_space=pl.ANY),
            ],
            out_specs=(
                pl.BlockSpec((columns, chunk), lambda i, s: (0, i * (chunks - 1))),
                pl.BlockSpec((columns, columns), full),
            ),
            scratch_shapes=[pltpu.VMEM((columns, 2 * (span + edge) + TILE), BF16)],
        ),
        input_output_aliases={7: 0},
        compiler_params=params,
        name="weigh_border",
    )(spots_of(near, (span + edge) // TILE), prior, snapshots, low, high, factor, gram, weighted)


def lanes_of(group, column):
    return jnp.broadcast_to(group[:, column:column + 1], (group.shape[0], TILE))


def row_of(group, row):
    return jnp.broadcast_to(group[row:row + 1, :], group.shape)


def eliminate(left, right, solved):
    groups = left.shape[0]
    sub = lax.broadcasted_iota(jnp.int32, (PANEL, TILE), 0)

    def panel(p, _):
        pivot, image = left[p], right[p]
        cols = [lanes_of(pivot, s) for s in range(PANEL)]
        d = [[row_of(cols[c], r) if r >= c else None for c in range(PANEL)] for r in range(PANEL)]
        rows_a = [row_of(pivot, r) for r in range(PANEL)]
        rows_n = [row_of(image, r) for r in range(PANEL)]
        inverse = []
        for s in range(PANEL):
            inverse.append(1.0 / d[s][s])
            for r in range(s + 1, PANEL):
                m = d[r][s] * inverse[s]
                for c in range(s + 1, r + 1):
                    d[r][c] = d[r][c] - m * d[c][s]
                rows_a[r] = rows_a[r] - m * rows_a[s]
                rows_n[r] = rows_n[r] - m * rows_n[s]
        for q in range(groups):
            fresh_a, fresh_n = left[q], right[q]
            work = [lanes_of(fresh_a, s) for s in range(PANEL)]
            for s in range(PANEL):
                factor = work[s] * inverse[s]
                for c in range(s + 1, PANEL):
                    work[c] = work[c] - factor * d[c][s]
                fresh_a = fresh_a - factor * rows_a[s]
                fresh_n = fresh_n - factor * rows_n[s]
            left[q] = pltpu.roll(fresh_a, TILE - PANEL, 1)
            right[q] = fresh_n
        merged = rows_n[0] * lax.rsqrt(d[0][0])
        for r in range(1, PANEL):
            merged = jnp.where(sub == r, rows_n[r] * lax.rsqrt(d[r][r]), merged)
        solved[p] = merged
        return 0

    lax.fori_loop(0, groups, panel, 0)


def reduce_gram(gram, left, right, solved):
    product = gram[:RANK]
    for _ in range(SUBSPACE_STEPS):
        image = jnp.dot(product, gram, precision=HIGHEST, preferred_element_type=F32)
        scale = 1.0 / jnp.sqrt(jnp.sum(product * image, axis=1, keepdims=True))
        normed = product * scale
        image = jnp.concatenate([image * scale, jnp.zeros((TILE - RANK, TILE), F32)], axis=0)
        inner = lax.dot_general(normed, image, NT, precision=HIGHEST, preferred_element_type=F32)
        left[...] = inner.reshape(left.shape)
        right[...] = normed.reshape(right.shape)
        eliminate(left, right, solved)
        weights = solved[...].reshape(RANK, TILE)
        product = jnp.dot(weights, gram, precision=HIGHEST, preferred_element_type=F32)
    lengths = jnp.sqrt(jnp.sum(product * product, axis=1, keepdims=True) + 1e-06)
    return (solved[...].reshape(RANK, TILE) * lengths).astype(BF16)


def inner_of(coefficients, gram):
    wide = coefficients.astype(F32)
    image = jnp.dot(wide, gram, precision=HIGHEST, preferred_element_type=F32)
    return lax.dot_general(image, wide, NT, precision=HIGHEST, preferred_element_type=F32)


def first_kernel(gram_ref, out_ref, own_ref, left, right, solved):
    gram = gram_ref[...]
    coefficients = reduce_gram(gram, left, right, solved)
    out_ref[...] = coefficients
    own_ref[...] = inner_of(coefficients, gram)


def merge_kernel(top_ref, upper_ref, out_ref, own_ref, left, right, solved):
    top = top_ref[...]
    bottom = jnp.concatenate([top.T[RANK:], upper_ref[...]], axis=1)
    gram = jnp.concatenate([top, bottom], axis=0)
    coefficients = reduce_gram(gram, left, right, solved)
    out_ref[...] = coefficients
    own_ref[...] = inner_of(coefficients, gram)


def compress(kernel, *gram):
    return pl.pallas_call(
        kernel,
        out_shape=(
            jax.ShapeDtypeStruct((RANK, gram[0].shape[1]), BF16),
            jax.ShapeDtypeStruct((RANK, RANK), F32),
        ),
        scratch_shapes=[pltpu.VMEM((RANK // PANEL, PANEL, TILE), F32)] * 3,
        compiler_params=pltpu.CompilerParams(vmem_limit_bytes=16 * 1024 * 1024),
        name="compress",
    )(*gram)


def combine(coefficients, rows):
    return jnp.dot(coefficients, rows, preferred_element_type=F32).astype(BF16)


def shared_out(rows, width, bit):
    pieces = [
        lax.dynamic_slice_in_dim(rows, (2 * pair + bit) * width, width, 1)
        for pair in range(rows.shape[1] // (2 * width))
    ]
    return pieces[0] if len(pieces) == 1 else jnp.concatenate(pieces, axis=1)


def ordered(upper_half, own_rows, partner_rows):
    lower_part = jnp.where(upper_half, partner_rows, own_rows)
    upper_part = jnp.where(upper_half, own_rows, partner_rows)
    return jnp.concatenate([lower_part, upper_part], axis=0)


def shards(snapshots, prior_basis, mass_factor, neighbours):
    stacked = jnp.concatenate([prior_basis, snapshots], axis=0)
    weighted, gram = weigh(prior_basis, snapshots, mass_factor, neighbours)
    members = lax.axis_size("tm")
    places = members * lax.axis_size("space")
    across = [1 << i for i in range(members.bit_length() - 1, places.bit_length() - 1)]
    coefficients, own = compress(first_kernel, total(gram, across))
    member = lax.axis_index("tm")
    width = stacked.shape[1] // members
    for level in range(members.bit_length() - 1):
        step = 1 << level
        bit = member // step % 2
        upper_half = bit == 1
        weighted = combine(coefficients, weighted)
        sent = swapped(shared_out(weighted, width, 1 - bit), step)
        partner_own = swapped(own, step)
        weighted = ordered(upper_half, shared_out(weighted, width, bit), sent)
        stacked = combine(coefficients, stacked)
        sent = swapped(shared_out(stacked, width, 1 - bit), step)
        stacked = ordered(upper_half, shared_out(stacked, width, bit), sent)
        top = lax.dot_general(weighted[:RANK], weighted, NT, preferred_element_type=F32)
        top = total(top, [1 << i for i in range(level + 1)] + across)
        coefficients, own = compress(merge_kernel, top, jnp.where(upper_half, own, partner_own))
    return combine(coefficients, stacked), combine(coefficients, weighted)


def solution(mesh):
    return jax.shard_map(
        shards,
        mesh=mesh,
        in_specs=(P("tm", "space"), P("tm", "space"), P(None, None, "space"), P("space", None)),
        out_specs=(P(None, ("space", "tm")), P(None, ("space", "tm"))),
        check_vma=False,
    )
```

```python
import functools
import jax
import jax.numpy as jnp
from jax import lax
from jax.experimental import pallas as pl
from jax.experimental.pallas import tpu as pltpu
from jax.sharding import PartitionSpec as P

BLOCK_DOFS = 64
RANK = 64
REACH = 8
SUBSPACE_STEPS = 3
PANEL = 8
TILE = 128
F32 = jnp.float32
BF16 = jnp.bfloat16
HIGHEST = lax.Precision.HIGHEST
NT = (((1,), (1,)), ((), ()))


def halo(parts, axis, width):
    count = lax.axis_size(axis)
    forward = [(i, i + 1) for i in range(count - 1)]
    backward = [(target, source) for source, target in forward]
    last = jnp.concatenate([part[:, part.shape[1] - width:] for part in parts], axis=0)
    first = jnp.concatenate([part[:, :width] for part in parts], axis=0)
    low = lax.ppermute(last, axis, forward)
    high = lax.ppermute(first, axis, backward)
    return low, high


def swapped(block, mask):
    axes = ("space", "tm")
    count = lax.axis_size("space") * lax.axis_size("tm")
    return lax.ppermute(block, axes, [(i, i ^ mask) for i in range(count)])


def total(block, bits):
    for start in range(0, len(bits), 2):
        first = bits[start]
        if start + 1 < len(bits):
            second = bits[start + 1]
            near, far, both = swapped(block, first), swapped(block, second), swapped(block, first | second)
            block = (block + near) + (far + both)
        else:
            block = block + swapped(block, first)
    return block


def fill_odd(bank, whole, block, start, stop):
    bank[:, whole + start + TILE:whole + stop] = bank[:, start + block:stop - block]


def weigh_chunk(neighbours_ref, row, shift, bank, factor_ref):
    neighbours, block, chunk = factor_ref.shape
    columns = bank.shape[0]
    tiles = (bank.shape[1] - TILE) // (2 * TILE)
    lower = lax.broadcasted_iota(jnp.int32, (columns, TILE), 1) < block

    def spot_of(k, line):
        place = neighbours_ref[k, line] - shift
        odd = place & 1
        return (place >> 1) + (odd * (tiles + 1) if k % 2 == 0 else (1 - odd) * tiles)

    pieces = []
    for tile in range(chunk // TILE):
        results = []
        for side in range(2):
            parts = []
            for k in range(neighbours):
                spot = spot_of(k, row + tile * 2 + side)
                parts.append(bank[:, pl.ds(pl.multiple_of(spot * TILE, TILE), TILE)])
            joined = [jnp.where(lower, parts[k], parts[k + 1]) for k in range(0, neighbours - 1, 2)]
            if neighbours % 2:
                joined.append(parts[-1][:, :block])
            results.append(jnp.concatenate(joined, axis=1))
        left = jnp.concatenate(results, axis=0)
        right = factor_ref[:, :, tile * TILE:(tile + 1) * TILE].reshape(neighbours * block, TILE)
        product = jnp.dot(left, right, preferred_element_type=F32)
        pieces.append(jnp.where(lower, product[:columns], product[columns:]).astype(BF16))
    return jnp.concatenate(pieces, axis=1)


def inside_kernel(edge, spots, prior_ref, snap_ref, factor_ref, weighted_ref, gram_ref, bank):
    step = pl.program_id(0)
    rows, width = prior_ref.shape
    _, block, chunk = factor_ref.shape
    whole = width + 2 * edge

    @pl.when(step == 0)
    def _():
        bank[:rows, edge:edge + width] = prior_ref[...]
        bank[rows:, edge:edge + width] = snap_ref[...]
        fill_odd(bank, whole, block, edge, edge + width)
        gram_ref[...] = jnp.zeros_like(gram_ref)

    shift = lax.axis_index("space") * (width // block) - edge // block
    weighted = weigh_chunk(spots, (step + 1) * (chunk // block), shift, bank, factor_ref)
    weighted_ref[...] = weighted
    gram_ref[...] += lax.dot_general(weighted, weighted, NT, preferred_element_type=F32)


def border_kernel(
    width, spots, prior_ref, snap_ref, low_ref, high_ref, factor_ref, part_ref, kept_ref, weighted_ref, gram_ref, bank
):
    step = pl.program_id(0)
    rows, span = prior_ref.shape
    edge = low_ref.shape[1]
    _, block, chunk = factor_ref.shape
    whole = span + edge

    @pl.when(step == 0)
    def _():
        bank[:, :edge] = low_ref[...]
        bank[:rows, edge:whole] = prior_ref[...]
        bank[rows:, edge:whole] = snap_ref[...]
        gram_ref[...] = part_ref[...]

    @pl.when(step != 0)
    def _():
        bank[:rows, :span] = prior_ref[...]
        bank[rows:, :span] = snap_ref[...]
        bank[:, span:whole] = high_ref[...]

    fill_odd(bank, whole, block, 0, whole)
    bank[:, whole + block:whole + TILE] = bank[:, :block]
    bank[:, 2 * whole:2 * whole + block] = bank[:, whole - block:whole]
    shift = lax.axis_index("space") * (width // block) - edge // block + step * ((width + 2 * edge - whole) // block)
    weighted = weigh_chunk(spots, step * ((width - chunk) // block), shift, bank, factor_ref)
    weighted_ref[...] = weighted
    gram_ref[...] += lax.dot_general(weighted, weighted, NT, preferred_element_type=F32)


def weigh(prior, snapshots, factor, neighbours):
    rows, width = prior.shape
    columns = 2 * rows
    count, block, _ = factor.shape
    edge = REACH * block
    chunk = 2 * edge
    span = 2 * chunk
    chunks = width // chunk
    low, high = halo((prior, snapshots), "space", edge)
    spots = neighbours.T
    full = lambda i, s: (0, 0)
    shapes = (
        jax.ShapeDtypeStruct((columns, width), BF16),
        jax.ShapeDtypeStruct((columns, columns), F32),
    )
    params = pltpu.CompilerParams(vmem_limit_bytes=56 * 1024 * 1024)
    weighted, gram = pl.pallas_call(
        functools.partial(inside_kernel, edge),
        out_shape=shapes,
        grid_spec=pltpu.PrefetchScalarGridSpec(
            num_scalar_prefetch=1,
            grid=(chunks - 2,),
            in_specs=[
                pl.BlockSpec((rows, width), full),
                pl.BlockSpec((rows, width), full),
                pl.BlockSpec((count, block, chunk), lambda i, s: (0, 0, i + 1)),
            ],
            out_specs=(
                pl.BlockSpec((columns, chunk), lambda i, s: (0, i + 1)),
                pl.BlockSpec((columns, columns), full),
            ),
            scratch_shapes=[pltpu.VMEM((columns, 2 * (width + 2 * edge) + TILE), BF16)],
        ),
        compiler_params=params,
        cost_estimate=pl.CostEstimate(
            flops=8 * columns * count * block * width, bytes_accessed=2 * factor.size, transcendentals=0
        ),
        name="weigh_inside",
    )(spots, prior, snapshots, factor)
    ends = width // span - 1
    return pl.pallas_call(
        functools.partial(border_kernel, width),
        out_shape=shapes,
        grid_spec=pltpu.PrefetchScalarGridSpec(
            num_scalar_prefetch=1,
            grid=(2,),
            in_specs=[
                pl.BlockSpec((rows, span), lambda i, s: (0, i * ends)),
                pl.BlockSpec((rows, span), lambda i, s: (0, i * ends)),
                pl.BlockSpec((columns, edge), full),
                pl.BlockSpec((columns, edge), full),
                pl.BlockSpec((count, block, chunk), lambda i, s: (0, 0, i * (chunks - 1))),
                pl.BlockSpec((columns, columns), full),
                pl.BlockSpec(memory_space=pl.ANY),
            ],
            out_specs=(
                pl.BlockSpec((columns, chunk), lambda i, s: (0, i * (chunks - 1))),
                pl.BlockSpec((columns, columns), full),
            ),
            scratch_shapes=[pltpu.VMEM((columns, 2 * (span + edge) + TILE), BF16)],
        ),
        input_output_aliases={7: 0},
        compiler_params=params,
        name="weigh_border",
    )(spots, prior, snapshots, low, high, factor, gram, weighted)


def lanes_of(group, column):
    return jnp.broadcast_to(group[:, column:column + 1], (group.shape[0], TILE))


def row_of(group, row):
    return jnp.broadcast_to(group[row:row + 1, :], group.shape)


def eliminate(left, right, solved):
    groups = left.shape[0]
    sub = lax.broadcasted_iota(jnp.int32, (PANEL, TILE), 0)

    for p in range(groups):
        pivot, image = left[p], right[p]
        cols = [lanes_of(pivot, PANEL * p + s) for s in range(PANEL)]
        d = [[row_of(cols[c], r) if r >= c else None for c in range(PANEL)] for r in range(PANEL)]
        rows_a = [row_of(pivot, r) for r in range(PANEL)]
        rows_n = [row_of(image, r) for r in range(PANEL)]
        inverse = []
        for s in range(PANEL):
            inverse.append(1.0 / d[s][s])
            for r in range(s + 1, PANEL):
                m = d[r][s] * inverse[s]
                for c in range(s + 1, r + 1):
                    d[r][c] = d[r][c] - m * d[c][s]
                rows_a[r] = rows_a[r] - m * rows_a[s]
                rows_n[r] = rows_n[r] - m * rows_n[s]
        for q in range(p + 1, groups):
            fresh_a, fresh_n = left[q], right[q]
            work = [lanes_of(fresh_a, PANEL * p + s) for s in range(PANEL)]
            for s in range(PANEL):
                factor = work[s] * inverse[s]
                for c in range(s + 1, PANEL):
                    work[c] = work[c] - factor * d[c][s]
                fresh_a = fresh_a - factor * rows_a[s]
                fresh_n = fresh_n - factor * rows_n[s]
            left[q] = fresh_a
            right[q] = fresh_n
        merged = rows_n[0] * lax.rsqrt(d[0][0])
        for r in range(1, PANEL):
            merged = jnp.where(sub == r, rows_n[r] * lax.rsqrt(d[r][r]), merged)
        solved[p] = merged


def reduce_gram(gram, left, right, solved):
    product = gram[:RANK]
    for _ in range(SUBSPACE_STEPS):
        image = jnp.dot(product, gram, precision=HIGHEST, preferred_element_type=F32)
        scale = 1.0 / jnp.sqrt(jnp.sum(product * image, axis=1, keepdims=True))
        normed = product * scale
        image = jnp.concatenate([image * scale, jnp.zeros((TILE - RANK, TILE), F32)], axis=0)
        inner = lax.dot_general(normed, image, NT, precision=HIGHEST, preferred_element_type=F32)
        left[...] = inner.reshape(left.shape)
        right[...] = normed.reshape(right.shape)
        eliminate(left, right, solved)
        weights = solved[...].reshape(RANK, TILE)
        product = jnp.dot(weights, gram, precision=HIGHEST, preferred_element_type=F32)
    lengths = jnp.sqrt(jnp.sum(product * product, axis=1, keepdims=True) + 1e-06)
    return (solved[...].reshape(RANK, TILE) * lengths).astype(BF16)


def inner_of(coefficients, gram):
    wide = coefficients.astype(F32)
    image = jnp.dot(wide, gram, precision=HIGHEST, preferred_element_type=F32)
    return lax.dot_general(image, wide, NT, precision=HIGHEST, preferred_element_type=F32)


def first_kernel(gram_ref, out_ref, own_ref, left, right, solved):
    gram = gram_ref[...]
    coefficients = reduce_gram(gram, left, right, solved)
    out_ref[...] = coefficients
    own_ref[...] = inner_of(coefficients, gram)


def merge_kernel(last, top_ref, upper_ref, out_ref, own_ref, left, right, solved):
    top = top_ref[...]
    bottom = jnp.concatenate([top.T[RANK:], upper_ref[...]], axis=1)
    gram = jnp.concatenate([top, bottom], axis=0)
    coefficients = reduce_gram(gram, left, right, solved)
    out_ref[...] = coefficients
    own_ref[...] = upper_ref[...] if last else inner_of(coefficients, gram)


def compress(kernel, *gram):
    return pl.pallas_call(
        kernel,
        out_shape=(
            jax.ShapeDtypeStruct((RANK, gram[0].shape[1]), BF16),
            jax.ShapeDtypeStruct((RANK, RANK), F32),
        ),
        scratch_shapes=[pltpu.VMEM((RANK // PANEL, PANEL, TILE), F32)] * 3,
        compiler_params=pltpu.CompilerParams(vmem_limit_bytes=16 * 1024 * 1024),
        name="compress",
    )(*gram)


def combine(coefficients, rows):
    return jnp.dot(coefficients, rows, preferred_element_type=F32).astype(BF16)


def combine_two(coefficients, first, second):
    rows = first.shape[0]
    return (
        jnp.dot(coefficients[:, :rows], first, preferred_element_type=F32)
        + jnp.dot(coefficients[:, rows:], second, preferred_element_type=F32)
    ).astype(BF16)


def shared_out(rows, width, bit):
    pieces = [
        lax.dynamic_slice_in_dim(rows, (2 * pair + bit) * width, width, 1)
        for pair in range(rows.shape[1] // (2 * width))
    ]
    return pieces[0] if len(pieces) == 1 else jnp.concatenate(pieces, axis=1)


def ordered(upper_half, own_rows, partner_rows):
    lower_part = jnp.where(upper_half, partner_rows, own_rows)
    upper_part = jnp.where(upper_half, own_rows, partner_rows)
    return jnp.concatenate([lower_part, upper_part], axis=0)


def shards(snapshots, prior_basis, mass_factor, neighbours):
    weighted, gram = weigh(prior_basis, snapshots, mass_factor, neighbours)
    members = lax.axis_size("tm")
    places = members * lax.axis_size("space")
    across = [1 << i for i in range(members.bit_length() - 1, places.bit_length() - 1)]
    coefficients, own = compress(first_kernel, total(gram, across))
    member = lax.axis_index("tm")
    width = snapshots.shape[1] // members
    for level in range(members.bit_length() - 1):
        step = 1 << level
        bit = member // step % 2
        upper_half = bit == 1
        weighted = combine(coefficients, weighted)
        sent = swapped(shared_out(weighted, width, 1 - bit), step)
        partner_own = swapped(own, step)
        weighted = ordered(upper_half, shared_out(weighted, width, bit), sent)
        if level == 0:
            stacked = combine_two(coefficients, prior_basis, snapshots)
        else:
            stacked = combine(coefficients, stacked)
        sent = swapped(shared_out(stacked, width, 1 - bit), step)
        stacked = ordered(upper_half, shared_out(stacked, width, bit), sent)
        top = lax.dot_general(weighted[:RANK], weighted, NT, preferred_element_type=F32)
        top = total(top, [1 << i for i in range(level + 1)] + across)
        coefficients, own = compress(functools.partial(merge_kernel, 2 * step == members), top, jnp.where(upper_half, own, partner_own))
    return combine(coefficients, stacked), combine(coefficients, weighted)


def solution(mesh):
    return jax.shard_map(
        shards,
        mesh=mesh,
        in_specs=(P("tm", "space"), P("tm", "space"), P(None, None, "space"), P("space", None)),
        out_specs=(P(None, ("space", "tm")), P(None, ("space", "tm"))),
        check_vma=False,
    )
```

```python
import functools
import jax
import jax.numpy as jnp
from jax import lax
from jax.experimental import pallas as pl
from jax.experimental.pallas import tpu as pltpu
from jax.sharding import PartitionSpec as P

BLOCK_DOFS = 64
RANK = 64
REACH = 8
SUBSPACE_STEPS = 3
PANEL = 8
TILE = 128
F32 = jnp.float32
BF16 = jnp.bfloat16
HIGHEST = lax.Precision.HIGHEST
NT = (((1,), (1,)), ((), ()))


def halo(parts, axis, width):
    count = lax.axis_size(axis)
    forward = [(i, i + 1) for i in range(count - 1)]
    backward = [(target, source) for source, target in forward]
    last = jnp.concatenate([part[:, part.shape[1] - width:] for part in parts], axis=0)
    first = jnp.concatenate([part[:, :width] for part in parts], axis=0)
    low = lax.ppermute(last, axis, forward)
    high = lax.ppermute(first, axis, backward)
    return low, high


def swapped(block, mask):
    axes = ("space", "tm")
    count = lax.axis_size("space") * lax.axis_size("tm")
    return lax.ppermute(block, axes, [(i, i ^ mask) for i in range(count)])


def total(block, bits):
    for start in range(0, len(bits), 2):
        first = bits[start]
        if start + 1 < len(bits):
            second = bits[start + 1]
            near, far, both = swapped(block, first), swapped(block, second), swapped(block, first | second)
            block = (block + near) + (far + both)
        else:
            block = block + swapped(block, first)
    return block


def fill_odd(bank, whole, block, start, stop):
    bank[:, whole + start + TILE:whole + stop] = bank[:, start + block:stop - block]


def weigh_chunk(neighbours_ref, row, shift, bank, factor_ref):
    neighbours, block, chunk = factor_ref.shape
    columns = bank.shape[0]
    tiles = (bank.shape[1] - TILE) // (2 * TILE)
    lower = lax.broadcasted_iota(jnp.int32, (columns, TILE), 1) < block

    def spot_of(k, line):
        place = neighbours_ref[k, line] - shift
        odd = place & 1
        return (place >> 1) + (odd * (tiles + 1) if k % 2 == 0 else (1 - odd) * tiles)

    pieces = []
    for tile in range(chunk // TILE):
        results = []
        for side in range(2):
            parts = []
            for k in range(neighbours):
                spot = spot_of(k, row + tile * 2 + side)
                parts.append(bank[:, pl.ds(pl.multiple_of(spot * TILE, TILE), TILE)])
            joined = [jnp.where(lower, parts[k], parts[k + 1]) for k in range(0, neighbours - 1, 2)]
            if neighbours % 2:
                joined.append(parts[-1][:, :block])
            results.append(jnp.concatenate(joined, axis=1))
        left = jnp.concatenate(results, axis=0)
        right = factor_ref[:, :, tile * TILE:(tile + 1) * TILE].reshape(neighbours * block, TILE)
        product = jnp.dot(left, right, preferred_element_type=F32)
        pieces.append(jnp.where(lower, product[:columns], product[columns:]).astype(BF16))
    return jnp.concatenate(pieces, axis=1)


def inside_kernel(edge, spots, prior_ref, snap_ref, factor_ref, weighted_ref, gram_ref, bank):
    step = pl.program_id(0)
    rows, width = prior_ref.shape
    _, block, chunk = factor_ref.shape
    whole = width + 2 * edge

    @pl.when(step == 0)
    def _():
        bank[:rows, edge:edge + width] = prior_ref[...]
        bank[rows:, edge:edge + width] = snap_ref[...]
        fill_odd(bank, whole, block, edge, edge + width)
        gram_ref[...] = jnp.zeros_like(gram_ref)

    shift = lax.axis_index("space") * (width // block) - edge // block
    weighted = weigh_chunk(spots, (step + 1) * (chunk // block), shift, bank, factor_ref)
    weighted_ref[...] = weighted
    gram_ref[...] += lax.dot_general(weighted, weighted, NT, preferred_element_type=F32)


def border_kernel(
    width, spots, prior_ref, snap_ref, low_ref, high_ref, factor_ref, part_ref, kept_ref, weighted_ref, gram_ref, bank
):
    step = pl.program_id(0)
    rows, span = prior_ref.shape
    edge = low_ref.shape[1]
    _, block, chunk = factor_ref.shape
    whole = span + edge

    @pl.when(step == 0)
    def _():
        bank[:, :edge] = low_ref[...]
        bank[:rows, edge:whole] = prior_ref[...]
        bank[rows:, edge:whole] = snap_ref[...]
        gram_ref[...] = part_ref[...]

    @pl.when(step != 0)
    def _():
        bank[:rows, :span] = prior_ref[...]
        bank[rows:, :span] = snap_ref[...]
        bank[:, span:whole] = high_ref[...]

    fill_odd(bank, whole, block, 0, whole)
    bank[:, whole + block:whole + TILE] = bank[:, :block]
    bank[:, 2 * whole:2 * whole + block] = bank[:, whole - block:whole]
    shift = lax.axis_index("space") * (width // block) - edge // block + step * ((width + 2 * edge - whole) // block)
    weighted = weigh_chunk(spots, step * ((width - chunk) // block), shift, bank, factor_ref)
    weighted_ref[...] = weighted
    gram_ref[...] += lax.dot_general(weighted, weighted, NT, preferred_element_type=F32)


def weigh(prior, snapshots, factor, neighbours):
    rows, width = prior.shape
    columns = 2 * rows
    count, block, _ = factor.shape
    edge = REACH * block
    chunk = 2 * edge
    span = 2 * chunk
    chunks = width // chunk
    low, high = halo((prior, snapshots), "space", edge)
    spots = neighbours.T
    full = lambda i, s: (0, 0)
    shapes = (
        jax.ShapeDtypeStruct((columns, width), BF16),
        jax.ShapeDtypeStruct((columns, columns), F32),
    )
    params = pltpu.CompilerParams(vmem_limit_bytes=24 * 1024 * 1024)
    weighted, gram = pl.pallas_call(
        functools.partial(inside_kernel, edge),
        out_shape=shapes,
        grid_spec=pltpu.PrefetchScalarGridSpec(
            num_scalar_prefetch=1,
            grid=(chunks - 2,),
            in_specs=[
                pl.BlockSpec((rows, width), full),
                pl.BlockSpec((rows, width), full),
                pl.BlockSpec((count, block, chunk), lambda i, s: (0, 0, i + 1)),
            ],
            out_specs=(
                pl.BlockSpec((columns, chunk), lambda i, s: (0, i + 1)),
                pl.BlockSpec((columns, columns), full),
            ),
            scratch_shapes=[pltpu.VMEM((columns, 2 * (width + 2 * edge) + TILE), BF16)],
        ),
        compiler_params=params,
        cost_estimate=pl.CostEstimate(
            flops=8 * columns * count * block * width, bytes_accessed=2 * factor.size, transcendentals=0
        ),
        name="weigh_inside",
    )(spots, prior, snapshots, factor)
    ends = width // span - 1
    return pl.pallas_call(
        functools.partial(border_kernel, width),
        out_shape=shapes,
        grid_spec=pltpu.PrefetchScalarGridSpec(
            num_scalar_prefetch=1,
            grid=(2,),
            in_specs=[
                pl.BlockSpec((rows, span), lambda i, s: (0, i * ends)),
                pl.BlockSpec((rows, span), lambda i, s: (0, i * ends)),
                pl.BlockSpec((columns, edge), full),
                pl.BlockSpec((columns, edge), full),
                pl.BlockSpec((count, block, chunk), lambda i, s: (0, 0, i * (chunks - 1))),
                pl.BlockSpec((columns, columns), full),
                pl.BlockSpec(memory_space=pl.ANY),
            ],
            out_specs=(
                pl.BlockSpec((columns, chunk), lambda i, s: (0, i * (chunks - 1))),
                pl.BlockSpec((columns, columns), full),
            ),
            scratch_shapes=[pltpu.VMEM((columns, 2 * (span + edge) + TILE), BF16)],
        ),
        input_output_aliases={7: 0},
        compiler_params=params,
        name="weigh_border",
    )(spots, prior, snapshots, low, high, factor, gram, weighted)


def lanes_of(group, column):
    return jnp.broadcast_to(group[:, column:column + 1], (group.shape[0], TILE))


def row_of(group, row):
    return jnp.broadcast_to(group[row:row + 1, :], group.shape)


def eliminate(left, right, solved):
    groups = left.shape[0]
    sub = lax.broadcasted_iota(jnp.int32, (PANEL, TILE), 0)

    for p in range(groups):
        pivot, image = left[p], right[p]
        cols = [lanes_of(pivot, PANEL * p + s) for s in range(PANEL)]
        d = [[row_of(cols[c], r) if r >= c else None for c in range(PANEL)] for r in range(PANEL)]
        rows_a = [row_of(pivot, r) for r in range(PANEL)]
        rows_n = [row_of(image, r) for r in range(PANEL)]
        inverse = []
        for s in range(PANEL):
            inverse.append(1.0 / d[s][s])
            for r in range(s + 1, PANEL):
                m = d[r][s] * inverse[s]
                for c in range(s + 1, r + 1):
                    d[r][c] = d[r][c] - m * d[c][s]
                rows_a[r] = rows_a[r] - m * rows_a[s]
                rows_n[r] = rows_n[r] - m * rows_n[s]
        for q in range(p + 1, groups):
            fresh_a, fresh_n = left[q], right[q]
            work = [lanes_of(fresh_a, PANEL * p + s) for s in range(PANEL)]
            for s in range(PANEL):
                factor = work[s] * inverse[s]
                for c in range(s + 1, PANEL):
                    work[c] = work[c] - factor * d[c][s]
                fresh_a = fresh_a - factor * rows_a[s]
                fresh_n = fresh_n - factor * rows_n[s]
            left[q] = fresh_a
            right[q] = fresh_n
        merged = rows_n[0] * lax.rsqrt(d[0][0])
        for r in range(1, PANEL):
            merged = jnp.where(sub == r, rows_n[r] * lax.rsqrt(d[r][r]), merged)
        solved[p] = merged


def reduce_gram(gram, left, right, solved):
    product = gram[:RANK]
    for _ in range(SUBSPACE_STEPS):
        image = jnp.dot(product, gram, precision=HIGHEST, preferred_element_type=F32)
        scale = 1.0 / jnp.sqrt(jnp.sum(product * image, axis=1, keepdims=True))
        normed = product * scale
        image = jnp.concatenate([image * scale, jnp.zeros((TILE - RANK, TILE), F32)], axis=0)
        inner = lax.dot_general(normed, image, NT, precision=HIGHEST, preferred_element_type=F32)
        left[...] = inner.reshape(left.shape)
        right[...] = normed.reshape(right.shape)
        eliminate(left, right, solved)
        weights = solved[...].reshape(RANK, TILE)
        product = jnp.dot(weights, gram, precision=HIGHEST, preferred_element_type=F32)
    lengths = jnp.sqrt(jnp.sum(product * product, axis=1, keepdims=True) + 1e-06)
    return (solved[...].reshape(RANK, TILE) * lengths).astype(BF16)


def inner_of(coefficients, gram):
    wide = coefficients.astype(F32)
    image = jnp.dot(wide, gram, precision=HIGHEST, preferred_element_type=F32)
    return lax.dot_general(image, wide, NT, precision=HIGHEST, preferred_element_type=F32)


def first_kernel(gram_ref, out_ref, own_ref, left, right, solved):
    gram = gram_ref[...]
    coefficients = reduce_gram(gram, left, right, solved)
    out_ref[...] = coefficients
    own_ref[...] = inner_of(coefficients, gram)


def merge_kernel(last, top_ref, upper_ref, out_ref, own_ref, left, right, solved):
    top = top_ref[...]
    bottom = jnp.concatenate([top.T[RANK:], upper_ref[...]], axis=1)
    gram = jnp.concatenate([top, bottom], axis=0)
    coefficients = reduce_gram(gram, left, right, solved)
    out_ref[...] = coefficients
    own_ref[...] = upper_ref[...] if last else inner_of(coefficients, gram)


def compress(kernel, *gram):
    return pl.pallas_call(
        kernel,
        out_shape=(
            jax.ShapeDtypeStruct((RANK, gram[0].shape[1]), BF16),
            jax.ShapeDtypeStruct((RANK, RANK), F32),
        ),
        scratch_shapes=[pltpu.VMEM((RANK // PANEL, PANEL, TILE), F32)] * 3,
        compiler_params=pltpu.CompilerParams(vmem_limit_bytes=16 * 1024 * 1024),
        name="compress",
    )(*gram)


def combine(coefficients, rows):
    return jnp.dot(coefficients, rows, preferred_element_type=F32).astype(BF16)


def shared_out(rows, width, bit):
    pieces = [
        lax.dynamic_slice_in_dim(rows, (2 * pair + bit) * width, width, 1)
        for pair in range(rows.shape[1] // (2 * width))
    ]
    return pieces[0] if len(pieces) == 1 else jnp.concatenate(pieces, axis=1)


def joined(parts, width, bit):
    return jnp.concatenate([shared_out(part, width, bit) for part in parts], axis=0)


def ordered(upper_half, own_rows, partner_rows):
    lower_part = jnp.where(upper_half, partner_rows, own_rows)
    upper_part = jnp.where(upper_half, own_rows, partner_rows)
    return jnp.concatenate([lower_part, upper_part], axis=0)


def shards(snapshots, prior_basis, mass_factor, neighbours):
    weighted, gram = weigh(prior_basis, snapshots, mass_factor, neighbours)
    members = lax.axis_size("tm")
    places = members * lax.axis_size("space")
    across = [1 << i for i in range(members.bit_length() - 1, places.bit_length() - 1)]
    member = lax.axis_index("tm")
    width = snapshots.shape[1] // members
    stacked = (prior_basis, snapshots)
    for level in range(members.bit_length() - 1):
        step = 1 << level
        bit = member // step % 2
        upper_half = bit == 1
        partner_weighted = swapped(shared_out(weighted, width, 1 - bit), step)
        own_weighted = shared_out(weighted, width, bit)
        if level == 0:
            partner_stacked = swapped(joined(stacked, width, 1 - bit), step)
            own_stacked = joined(stacked, width, bit)
            coefficients, own = compress(first_kernel, total(gram, across))
        else:
            partner_stacked = swapped(shared_out(stacked, width, 1 - bit), step)
            own_stacked = shared_out(stacked, width, bit)
            coefficients, own = compress(functools.partial(merge_kernel, False), top, upper)
        partner_coefficients = swapped(coefficients, step)
        partner_own = swapped(own, step)
        weighted = ordered(
            upper_half, combine(coefficients, own_weighted), combine(partner_coefficients, partner_weighted)
        )
        top = lax.dot_general(weighted[:RANK], weighted, NT, preferred_element_type=F32)
        top = total(top, [1 << i for i in range(level + 1)] + across)
        upper = jnp.where(upper_half, own, partner_own)
        stacked = ordered(
            upper_half, combine(coefficients, own_stacked), combine(partner_coefficients, partner_stacked)
        )
    coefficients, _ = compress(functools.partial(merge_kernel, True), top, upper)
    return combine(coefficients, stacked), combine(coefficients, weighted)


def solution(mesh):
    return jax.shard_map(
        shards,
        mesh=mesh,
        in_specs=(P("tm", "space"), P("tm", "space"), P(None, None, "space"), P("space", None)),
        out_specs=(P(None, ("space", "tm")), P(None, ("space", "tm"))),
        check_vma=False,
    )
```

```python
import functools
import jax
import jax.numpy as jnp
from jax import lax
from jax.experimental import pallas as pl
from jax.experimental.pallas import tpu as pltpu
from jax.sharding import PartitionSpec as P

BLOCK_DOFS = 64
RANK = 64
REACH = 8
SUBSPACE_STEPS = 3
PANEL = 8
TILE = 128
F32 = jnp.float32
BF16 = jnp.bfloat16
HIGHEST = lax.Precision.HIGHEST
NT = (((1,), (1,)), ((), ()))


def halo(parts, axis, width):
    count = lax.axis_size(axis)
    forward = [(i, i + 1) for i in range(count - 1)]
    backward = [(target, source) for source, target in forward]
    last = jnp.concatenate([part[:, part.shape[1] - width:] for part in parts], axis=0)
    first = jnp.concatenate([part[:, :width] for part in parts], axis=0)
    low = lax.ppermute(last, axis, forward)
    high = lax.ppermute(first, axis, backward)
    return low, high


def swapped(block, mask):
    axes = ("space", "tm")
    count = lax.axis_size("space") * lax.axis_size("tm")
    return lax.ppermute(block, axes, [(i, i ^ mask) for i in range(count)])


def total(block, bits):
    for start in range(0, len(bits), 2):
        first = bits[start]
        if start + 1 < len(bits):
            second = bits[start + 1]
            near, far, both = swapped(block, first), swapped(block, second), swapped(block, first | second)
            block = (block + near) + (far + both)
        else:
            block = block + swapped(block, first)
    return block


def fill_odd(bank, whole, block, start, stop):
    bank[:, whole + start + TILE:whole + stop] = bank[:, start + block:stop - block]


def weigh_chunk(neighbours_ref, row, shift, bank, factor_ref):
    neighbours, block, chunk = factor_ref.shape
    columns = bank.shape[0]
    tiles = (bank.shape[1] - TILE) // (2 * TILE)
    lower = lax.broadcasted_iota(jnp.int32, (columns, TILE), 1) < block

    def spot_of(k, line):
        place = neighbours_ref[k, line] - shift
        odd = place & 1
        return (place >> 1) + (odd * (tiles + 1) if k % 2 == 0 else (1 - odd) * tiles)

    pieces = []
    for tile in range(chunk // TILE):
        results = []
        for side in range(2):
            parts = []
            for k in range(neighbours):
                spot = spot_of(k, row + tile * 2 + side)
                parts.append(bank[:, pl.ds(pl.multiple_of(spot * TILE, TILE), TILE)])
            joined = [jnp.where(lower, parts[k], parts[k + 1]) for k in range(0, neighbours - 1, 2)]
            if neighbours % 2:
                joined.append(parts[-1][:, :block])
            results.append(jnp.concatenate(joined, axis=1))
        left = jnp.concatenate(results, axis=0)
        right = factor_ref[:, :, tile * TILE:(tile + 1) * TILE].reshape(neighbours * block, TILE)
        product = jnp.dot(left, right, preferred_element_type=F32)
        pieces.append(jnp.where(lower, product[:columns], product[columns:]).astype(BF16))
    return jnp.concatenate(pieces, axis=1)


def fetch(factor_ref, start, fetched, arrived, step):
    chunk = fetched.shape[3]
    piece = factor_ref.at[:, :, pl.ds(pl.multiple_of(start, TILE), chunk)]
    return pltpu.make_async_copy(piece, fetched.at[step], arrived.at[step])


def inside_kernel(edge, spots, prior_ref, snap_ref, factor_ref, weighted_ref, gram_ref, bank, fetched, arrived):
    step = pl.program_id(0)
    rows, width = prior_ref.shape
    steps, _, block, chunk = fetched.shape
    whole = width + 2 * edge

    @pl.when(step == 0)
    def _():
        for i in range(steps):
            fetch(factor_ref, (i + 1) * chunk, fetched, arrived, i).start()
        bank[:rows, edge:edge + width] = prior_ref[...]
        bank[rows:, edge:edge + width] = snap_ref[...]
        fill_odd(bank, whole, block, edge, edge + width)
        gram_ref[...] = jnp.zeros_like(gram_ref)

    shift = lax.axis_index("space") * (width // block) - edge // block
    fetch(factor_ref, (step + 1) * chunk, fetched, arrived, step).wait()
    weighted = weigh_chunk(spots, (step + 1) * (chunk // block), shift, bank, fetched.at[step])
    weighted_ref[...] = weighted
    gram_ref[...] += lax.dot_general(weighted, weighted, NT, preferred_element_type=F32)


def border_kernel(
    width, spots, prior_ref, snap_ref, low_ref, high_ref, factor_ref, part_ref, kept_ref, weighted_ref, gram_ref, bank,
    fetched, arrived,
):
    step = pl.program_id(0)
    rows, span = prior_ref.shape
    edge = low_ref.shape[1]
    steps, _, block, chunk = fetched.shape
    whole = span + edge

    @pl.when(step == 0)
    def _():
        for i in range(steps):
            fetch(factor_ref, i * (width - chunk), fetched, arrived, i).start()
        bank[:, :edge] = low_ref[...]
        bank[:rows, edge:whole] = prior_ref[...]
        bank[rows:, edge:whole] = snap_ref[...]
        gram_ref[...] = part_ref[...]

    @pl.when(step != 0)
    def _():
        bank[:rows, :span] = prior_ref[...]
        bank[rows:, :span] = snap_ref[...]
        bank[:, span:whole] = high_ref[...]

    fill_odd(bank, whole, block, 0, whole)
    bank[:, whole + block:whole + TILE] = bank[:, :block]
    bank[:, 2 * whole:2 * whole + block] = bank[:, whole - block:whole]
    shift = lax.axis_index("space") * (width // block) - edge // block + step * ((width + 2 * edge - whole) // block)
    fetch(factor_ref, step * (width - chunk), fetched, arrived, step).wait()
    weighted = weigh_chunk(spots, step * ((width - chunk) // block), shift, bank, fetched.at[step])
    weighted_ref[...] = weighted
    gram_ref[...] += lax.dot_general(weighted, weighted, NT, preferred_element_type=F32)


def weigh(prior, snapshots, factor, neighbours):
    rows, width = prior.shape
    columns = 2 * rows
    count, block, _ = factor.shape
    edge = REACH * block
    chunk = 2 * edge
    span = 2 * chunk
    chunks = width // chunk
    low, high = halo((prior, snapshots), "space", edge)
    spots = neighbours.T
    full = lambda i, s: (0, 0)
    fetching = lambda steps: [
        pltpu.VMEM((steps, count, block, chunk), BF16), pltpu.SemaphoreType.DMA((steps,))
    ]
    shapes = (
        jax.ShapeDtypeStruct((columns, width), BF16),
        jax.ShapeDtypeStruct((columns, columns), F32),
    )
    params = pltpu.CompilerParams(vmem_limit_bytes=56 * 1024 * 1024)
    weighted, gram = pl.pallas_call(
        functools.partial(inside_kernel, edge),
        out_shape=shapes,
        grid_spec=pltpu.PrefetchScalarGridSpec(
            num_scalar_prefetch=1,
            grid=(chunks - 2,),
            in_specs=[
                pl.BlockSpec((rows, width), full),
                pl.BlockSpec((rows, width), full),
                pl.BlockSpec(memory_space=pl.ANY),
            ],
            out_specs=(
                pl.BlockSpec((columns, chunk), lambda i, s: (0, i + 1)),
                pl.BlockSpec((columns, columns), full),
            ),
            scratch_shapes=[pltpu.VMEM((columns, 2 * (width + 2 * edge) + TILE), BF16)] + fetching(chunks - 2),
        ),
        compiler_params=params,
        cost_estimate=pl.CostEstimate(
            flops=8 * columns * count * block * width, bytes_accessed=2 * factor.size, transcendentals=0
        ),
        name="weigh_inside",
    )(spots, prior, snapshots, factor)
    ends = width // span - 1
    return pl.pallas_call(
        functools.partial(border_kernel, width),
        out_shape=shapes,
        grid_spec=pltpu.PrefetchScalarGridSpec(
            num_scalar_prefetch=1,
            grid=(2,),
            in_specs=[
                pl.BlockSpec((rows, span), lambda i, s: (0, i * ends)),
                pl.BlockSpec((rows, span), lambda i, s: (0, i * ends)),
                pl.BlockSpec((columns, edge), full),
                pl.BlockSpec((columns, edge), full),
                pl.BlockSpec(memory_space=pl.ANY),
                pl.BlockSpec((columns, columns), full),
                pl.BlockSpec(memory_space=pl.ANY),
            ],
            out_specs=(
                pl.BlockSpec((columns, chunk), lambda i, s: (0, i * (chunks - 1))),
                pl.BlockSpec((columns, columns), full),
            ),
            scratch_shapes=[pltpu.VMEM((columns, 2 * (span + edge) + TILE), BF16)] + fetching(2),
        ),
        input_output_aliases={7: 0},
        compiler_params=params,
        name="weigh_border",
    )(spots, prior, snapshots, low, high, factor, gram, weighted)


def lanes_of(group, column):
    return jnp.broadcast_to(group[:, column:column + 1], (group.shape[0], TILE))


def row_of(group, row):
    return jnp.broadcast_to(group[row:row + 1, :], group.shape)


def eliminate(left, right, solved):
    groups = left.shape[0]
    sub = lax.broadcasted_iota(jnp.int32, (PANEL, TILE), 0)

    for p in range(groups):
        pivot, image = left[p], right[p]
        cols = [lanes_of(pivot, PANEL * p + s) for s in range(PANEL)]
        d = [[row_of(cols[c], r) if r >= c else None for c in range(PANEL)] for r in range(PANEL)]
        rows_a = [row_of(pivot, r) for r in range(PANEL)]
        rows_n = [row_of(image, r) for r in range(PANEL)]
        inverse = []
        for s in range(PANEL):
            inverse.append(1.0 / d[s][s])
            for r in range(s + 1, PANEL):
                m = d[r][s] * inverse[s]
                for c in range(s + 1, r + 1):
                    d[r][c] = d[r][c] - m * d[c][s]
                rows_a[r] = rows_a[r] - m * rows_a[s]
                rows_n[r] = rows_n[r] - m * rows_n[s]
        for q in range(p + 1, groups):
            fresh_a, fresh_n = left[q], right[q]
            work = [lanes_of(fresh_a, PANEL * p + s) for s in range(PANEL)]
            for s in range(PANEL):
                factor = work[s] * inverse[s]
                for c in range(s + 1, PANEL):
                    work[c] = work[c] - factor * d[c][s]
                fresh_a = fresh_a - factor * rows_a[s]
                fresh_n = fresh_n - factor * rows_n[s]
            left[q] = fresh_a
            right[q] = fresh_n
        merged = rows_n[0] * lax.rsqrt(d[0][0])
        for r in range(1, PANEL):
            merged = jnp.where(sub == r, rows_n[r] * lax.rsqrt(d[r][r]), merged)
        solved[p] = merged


def reduce_gram(gram, left, right, solved):
    product = gram[:RANK]
    for _ in range(SUBSPACE_STEPS):
        image = jnp.dot(product, gram, precision=HIGHEST, preferred_element_type=F32)
        scale = 1.0 / jnp.sqrt(jnp.sum(product * image, axis=1, keepdims=True))
        normed = product * scale
        image = jnp.concatenate([image * scale, jnp.zeros((TILE - RANK, TILE), F32)], axis=0)
        inner = lax.dot_general(normed, image, NT, precision=HIGHEST, preferred_element_type=F32)
        left[...] = inner.reshape(left.shape)
        right[...] = normed.reshape(right.shape)
        eliminate(left, right, solved)
        weights = solved[...].reshape(RANK, TILE)
        product = jnp.dot(weights, gram, precision=HIGHEST, preferred_element_type=F32)
    lengths = jnp.sqrt(jnp.sum(product * product, axis=1, keepdims=True) + 1e-06)
    return (solved[...].reshape(RANK, TILE) * lengths).astype(BF16)


def inner_of(coefficients, gram):
    wide = coefficients.astype(F32)
    image = jnp.dot(wide, gram, precision=HIGHEST, preferred_element_type=F32)
    return lax.dot_general(image, wide, NT, precision=HIGHEST, preferred_element_type=F32)


def first_kernel(gram_ref, out_ref, own_ref, left, right, solved):
    gram = gram_ref[...]
    coefficients = reduce_gram(gram, left, right, solved)
    out_ref[...] = coefficients
    own_ref[...] = inner_of(coefficients, gram)


def merge_kernel(last, top_ref, upper_ref, out_ref, own_ref, left, right, solved):
    top = top_ref[...]
    bottom = jnp.concatenate([top.T[RANK:], upper_ref[...]], axis=1)
    gram = jnp.concatenate([top, bottom], axis=0)
    coefficients = reduce_gram(gram, left, right, solved)
    out_ref[...] = coefficients
    own_ref[...] = upper_ref[...] if last else inner_of(coefficients, gram)


def compress(kernel, *gram):
    return pl.pallas_call(
        kernel,
        out_shape=(
            jax.ShapeDtypeStruct((RANK, gram[0].shape[1]), BF16),
            jax.ShapeDtypeStruct((RANK, RANK), F32),
        ),
        scratch_shapes=[pltpu.VMEM((RANK // PANEL, PANEL, TILE), F32)] * 3,
        compiler_params=pltpu.CompilerParams(vmem_limit_bytes=16 * 1024 * 1024),
        name="compress",
    )(*gram)


def combine(coefficients, rows):
    return jnp.dot(coefficients, rows, preferred_element_type=F32).astype(BF16)


def combine_two(coefficients, first, second):
    rows = first.shape[0]
    return (
        jnp.dot(coefficients[:, :rows], first, preferred_element_type=F32)
        + jnp.dot(coefficients[:, rows:], second, preferred_element_type=F32)
    ).astype(BF16)


def shared_out(rows, width, bit):
    pieces = [
        lax.dynamic_slice_in_dim(rows, (2 * pair + bit) * width, width, 1)
        for pair in range(rows.shape[1] // (2 * width))
    ]
    return pieces[0] if len(pieces) == 1 else jnp.concatenate(pieces, axis=1)


def ordered(upper_half, own_rows, partner_rows):
    lower_part = jnp.where(upper_half, partner_rows, own_rows)
    upper_part = jnp.where(upper_half, own_rows, partner_rows)
    return jnp.concatenate([lower_part, upper_part], axis=0)


def shards(snapshots, prior_basis, mass_factor, neighbours):
    weighted, gram = weigh(prior_basis, snapshots, mass_factor, neighbours)
    members = lax.axis_size("tm")
    places = members * lax.axis_size("space")
    across = [1 << i for i in range(members.bit_length() - 1, places.bit_length() - 1)]
    member = lax.axis_index("tm")
    width = snapshots.shape[1] // members
    partner_weighted = None
    coefficients, own = compress(first_kernel, total(gram, across))
    for level in range(members.bit_length() - 1):
        step = 1 << level
        bit = member // step % 2
        upper_half = bit == 1
        partner_own = swapped(own, step)
        if partner_weighted is None:
            weighted = combine(coefficients, weighted)
            partner_weighted = swapped(shared_out(weighted, width, 1 - bit), step)
            own_weighted = shared_out(weighted, width, bit)
        else:
            partner_weighted = combine(swapped(coefficients, step), partner_weighted)
            own_weighted = combine(coefficients, shared_out(weighted, width, bit))
        weighted = ordered(upper_half, own_weighted, partner_weighted)
        if level == 0:
            stacked = combine_two(coefficients, prior_basis, snapshots)
        else:
            stacked = combine(coefficients, stacked)
        partner_stacked = swapped(shared_out(stacked, width, 1 - bit), step)
        stacked = ordered(upper_half, shared_out(stacked, width, bit), partner_stacked)
        top = lax.dot_general(weighted[:RANK], weighted, NT, preferred_element_type=F32)
        last = 2 * step == members
        if not last:
            next_bit = member // (2 * step) % 2
            partner_weighted = swapped(shared_out(weighted, width, 1 - next_bit), 2 * step)
        top = total(top, [1 << i for i in range(level + 1)] + across)
        upper = jnp.where(upper_half, own, partner_own)
        coefficients, own = compress(functools.partial(merge_kernel, last), top, upper)
    return combine(coefficients, stacked), combine(coefficients, weighted)


def solution(mesh):
    return jax.shard_map(
        shards,
        mesh=mesh,
        in_specs=(P("tm", "space"), P("tm", "space"), P(None, None, "space"), P("space", None)),
        out_specs=(P(None, ("space", "tm")), P(None, ("space", "tm"))),
        check_vma=False,
    )
```

```python
import functools
import jax
import jax.numpy as jnp
from jax import lax
from jax.experimental import pallas as pl
from jax.experimental.pallas import tpu as pltpu
from jax.sharding import PartitionSpec as P

BLOCK_DOFS = 64
RANK = 64
REACH = 8
SUBSPACE_STEPS = 3
PANEL = 8
TILE = 128
F32 = jnp.float32
BF16 = jnp.bfloat16
HIGHEST = lax.Precision.HIGHEST
NT = (((1,), (1,)), ((), ()))


def halo(parts, axis, width):
    count = lax.axis_size(axis)
    forward = [(i, i + 1) for i in range(count - 1)]
    backward = [(target, source) for source, target in forward]
    last = jnp.concatenate([part[:, part.shape[1] - width:] for part in parts], axis=0)
    first = jnp.concatenate([part[:, :width] for part in parts], axis=0)
    low = lax.ppermute(last, axis, forward)
    high = lax.ppermute(first, axis, backward)
    return low, high


def swapped(block, mask):
    axes = ("space", "tm")
    count = lax.axis_size("space") * lax.axis_size("tm")
    return lax.ppermute(block, axes, [(i, i ^ mask) for i in range(count)])


def total(block, bits, stage):
    for start in range(0, len(bits), stage):
        first = bits[start]
        if stage == 2 and start + 1 < len(bits):
            second = bits[start + 1]
            near, far, both = swapped(block, first), swapped(block, second), swapped(block, first | second)
            block = (block + near) + (far + both)
        else:
            block = block + swapped(block, first)
    return block


def fill_odd(bank, whole, block, start, stop):
    bank[:, whole + start + TILE:whole + stop] = bank[:, start + block:stop - block]


def weigh_chunk(neighbours_ref, row, shift, bank, factor_ref):
    neighbours, block, chunk = factor_ref.shape
    columns = bank.shape[0]
    tiles = (bank.shape[1] - TILE) // (2 * TILE)
    lower = lax.broadcasted_iota(jnp.int32, (columns, TILE), 1) < block

    def spot_of(k, line):
        place = neighbours_ref[k, line] - shift
        odd = place & 1
        return (place >> 1) + (odd * (tiles + 1) if k % 2 == 0 else (1 - odd) * tiles)

    pieces = []
    for tile in range(chunk // TILE):
        results = []
        for side in range(2):
            parts = []
            for k in range(neighbours):
                spot = spot_of(k, row + tile * 2 + side)
                parts.append(bank[:, pl.ds(pl.multiple_of(spot * TILE, TILE), TILE)])
            joined = [jnp.where(lower, parts[k], parts[k + 1]) for k in range(0, neighbours - 1, 2)]
            if neighbours % 2:
                joined.append(parts[-1][:, :block])
            results.append(jnp.concatenate(joined, axis=1))
        left = jnp.concatenate(results, axis=0)
        right = factor_ref[:, :, tile * TILE:(tile + 1) * TILE].reshape(neighbours * block, TILE)
        product = jnp.dot(left, right, preferred_element_type=F32)
        pieces.append(jnp.where(lower, product[:columns], product[columns:]).astype(BF16))
    return jnp.concatenate(pieces, axis=1)


def fetch(factor_ref, start, fetched, arrived, step):
    chunk = fetched.shape[3]
    piece = factor_ref.at[:, :, pl.ds(pl.multiple_of(start, TILE), chunk)]
    return pltpu.make_async_copy(piece, fetched.at[step], arrived.at[step])


def inside_kernel(edge, spots, prior_ref, snap_ref, factor_ref, weighted_ref, gram_ref, bank, fetched, arrived):
    step = pl.program_id(0)
    rows, width = prior_ref.shape
    steps, _, block, chunk = fetched.shape
    whole = width + 2 * edge

    @pl.when(step == 0)
    def _():
        for i in range(steps):
            fetch(factor_ref, (i + 1) * chunk, fetched, arrived, i).start()
        bank[:rows, edge:edge + width] = prior_ref[...]
        bank[rows:, edge:edge + width] = snap_ref[...]
        fill_odd(bank, whole, block, edge, edge + width)
        gram_ref[...] = jnp.zeros_like(gram_ref)

    shift = lax.axis_index("space") * (width // block) - edge // block
    fetch(factor_ref, (step + 1) * chunk, fetched, arrived, step).wait()
    weighted = weigh_chunk(spots, (step + 1) * (chunk // block), shift, bank, fetched.at[step])
    weighted_ref[...] = weighted
    gram_ref[...] += lax.dot_general(weighted, weighted, NT, preferred_element_type=F32)


def packed(gram):
    half = gram.shape[0] // 2
    quarter = half // 2
    corner = gram[half:, half:]
    return jnp.concatenate([gram[:half], jnp.concatenate([corner[:quarter], corner[quarter:]], axis=1)], axis=0)


def unpacked(blocks):
    half = blocks.shape[1] // 2
    top, pair = blocks[:half], blocks[half:]
    corner = jnp.concatenate([pair[:, :half], pair[:, half:]], axis=0)
    return whole_of(top, corner)


def whole_of(top, corner):
    half = top.shape[0]
    return jnp.concatenate([top, jnp.concatenate([top.T[half:], corner], axis=1)], axis=0)


def border_kernel(
    width, spots, prior_ref, snap_ref, low_ref, high_ref, factor_ref, part_ref, kept_ref, weighted_ref, packed_ref, bank, gram
):
    step = pl.program_id(0)
    rows, span = prior_ref.shape
    edge = low_ref.shape[1]
    _, block, chunk = factor_ref.shape
    whole = span + edge

    @pl.when(step == 0)
    def _():
        bank[:, :edge] = low_ref[...]
        bank[:rows, edge:whole] = prior_ref[...]
        bank[rows:, edge:whole] = snap_ref[...]
        gram[...] = part_ref[...]

    @pl.when(step != 0)
    def _():
        bank[:rows, :span] = prior_ref[...]
        bank[rows:, :span] = snap_ref[...]
        bank[:, span:whole] = high_ref[...]

    fill_odd(bank, whole, block, 0, whole)
    bank[:, whole + block:whole + TILE] = bank[:, :block]
    bank[:, 2 * whole:2 * whole + block] = bank[:, whole - block:whole]
    shift = lax.axis_index("space") * (width // block) - edge // block + step * ((width + 2 * edge - whole) // block)
    weighted = weigh_chunk(spots, step * ((width - chunk) // block), shift, bank, factor_ref)
    weighted_ref[...] = weighted
    gram[...] += lax.dot_general(weighted, weighted, NT, preferred_element_type=F32)

    @pl.when(step == pl.num_programs(0) - 1)
    def _():
        packed_ref[...] = packed(gram[...])


def weigh(prior, snapshots, factor, neighbours):
    rows, width = prior.shape
    columns = 2 * rows
    count, block, _ = factor.shape
    edge = REACH * block
    chunk = 2 * edge
    span = 2 * chunk
    chunks = width // chunk
    low, high = halo((prior, snapshots), "space", edge)
    spots = neighbours.T
    full = lambda i, s: (0, 0)
    fetching = lambda steps: [
        pltpu.VMEM((steps, count, block, chunk), BF16), pltpu.SemaphoreType.DMA((steps,))
    ]
    shapes = (
        jax.ShapeDtypeStruct((columns, width), BF16),
        jax.ShapeDtypeStruct((columns, columns), F32),
    )
    params = pltpu.CompilerParams(vmem_limit_bytes=56 * 1024 * 1024)
    weighted, gram = pl.pallas_call(
        functools.partial(inside_kernel, edge),
        out_shape=shapes,
        grid_spec=pltpu.PrefetchScalarGridSpec(
            num_scalar_prefetch=1,
            grid=(chunks - 2,),
            in_specs=[
                pl.BlockSpec((rows, width), full),
                pl.BlockSpec((rows, width), full),
                pl.BlockSpec(memory_space=pl.ANY),
            ],
            out_specs=(
                pl.BlockSpec((columns, chunk), lambda i, s: (0, i + 1)),
                pl.BlockSpec((columns, columns), full),
            ),
            scratch_shapes=[pltpu.VMEM((columns, 2 * (width + 2 * edge) + TILE), BF16)] + fetching(chunks - 2),
        ),
        compiler_params=params,
        cost_estimate=pl.CostEstimate(
            flops=8 * columns * count * block * width, bytes_accessed=2 * factor.size, transcendentals=0
        ),
        name="weigh_inside",
    )(spots, prior, snapshots, factor)
    ends = width // span - 1
    return pl.pallas_call(
        functools.partial(border_kernel, width),
        out_shape=(shapes[0], jax.ShapeDtypeStruct((columns * 3 // 4, columns), F32)),
        grid_spec=pltpu.PrefetchScalarGridSpec(
            num_scalar_prefetch=1,
            grid=(2,),
            in_specs=[
                pl.BlockSpec((rows, span), lambda i, s: (0, i * ends)),
                pl.BlockSpec((rows, span), lambda i, s: (0, i * ends)),
                pl.BlockSpec((columns, edge), full),
                pl.BlockSpec((columns, edge), full),
                pl.BlockSpec((count, block, chunk), lambda i, s: (0, 0, i * (chunks - 1))),
                pl.BlockSpec((columns, columns), full),
                pl.BlockSpec(memory_space=pl.ANY),
            ],
            out_specs=(
                pl.BlockSpec((columns, chunk), lambda i, s: (0, i * (chunks - 1))),
                pl.BlockSpec((columns * 3 // 4, columns), full),
            ),
            scratch_shapes=[
                pltpu.VMEM((columns, 2 * (span + edge) + TILE), BF16),
                pltpu.VMEM((columns, columns), F32),
            ],
        ),
        input_output_aliases={7: 0},
        compiler_params=params,
        name="weigh_border",
    )(spots, prior, snapshots, low, high, factor, gram, weighted)


def lanes_of(group, column):
    return jnp.broadcast_to(group[:, column:column + 1], (group.shape[0], TILE))


def row_of(group, row):
    return jnp.broadcast_to(group[row:row + 1, :], group.shape)


def eliminate(left, right, solved):
    groups = left.shape[0]
    sub = lax.broadcasted_iota(jnp.int32, (PANEL, TILE), 0)

    for p in range(groups):
        pivot, image = left[p], right[p]
        cols = [lanes_of(pivot, PANEL * p + s) for s in range(PANEL)]
        d = [[row_of(cols[c], r) if r >= c else None for c in range(PANEL)] for r in range(PANEL)]
        rows_a = [row_of(pivot, r) for r in range(PANEL)]
        rows_n = [row_of(image, r) for r in range(PANEL)]
        inverse = []
        for s in range(PANEL):
            inverse.append(1.0 / d[s][s])
            for r in range(s + 1, PANEL):
                m = d[r][s] * inverse[s]
                for c in range(s + 1, r + 1):
                    d[r][c] = d[r][c] - m * d[c][s]
                rows_a[r] = rows_a[r] - m * rows_a[s]
                rows_n[r] = rows_n[r] - m * rows_n[s]
        for q in range(p + 1, groups):
            fresh_a, fresh_n = left[q], right[q]
            work = [lanes_of(fresh_a, PANEL * p + s) for s in range(PANEL)]
            for s in range(PANEL):
                factor = work[s] * inverse[s]
                for c in range(s + 1, PANEL):
                    work[c] = work[c] - factor * d[c][s]
                fresh_a = fresh_a - factor * rows_a[s]
                fresh_n = fresh_n - factor * rows_n[s]
            left[q] = fresh_a
            right[q] = fresh_n
        merged = rows_n[0] * lax.rsqrt(d[0][0])
        for r in range(1, PANEL):
            merged = jnp.where(sub == r, rows_n[r] * lax.rsqrt(d[r][r]), merged)
        solved[p] = merged


def reduce_gram(gram, left, right, solved):
    product = gram[:RANK]
    for _ in range(SUBSPACE_STEPS):
        image = jnp.dot(product, gram, precision=HIGHEST, preferred_element_type=F32)
        scale = 1.0 / jnp.sqrt(jnp.sum(product * image, axis=1, keepdims=True))
        normed = product * scale
        image = jnp.concatenate([image * scale, jnp.zeros((TILE - RANK, TILE), F32)], axis=0)
        inner = lax.dot_general(normed, image, NT, precision=HIGHEST, preferred_element_type=F32)
        left[...] = inner.reshape(left.shape)
        right[...] = normed.reshape(right.shape)
        eliminate(left, right, solved)
        weights = solved[...].reshape(RANK, TILE)
        product = jnp.dot(weights, gram, precision=HIGHEST, preferred_element_type=F32)
    lengths = jnp.sqrt(jnp.sum(product * product, axis=1, keepdims=True) + 1e-06)
    return (solved[...].reshape(RANK, TILE) * lengths).astype(BF16)


def inner_of(coefficients, gram):
    wide = coefficients.astype(F32)
    image = jnp.dot(wide, gram, precision=HIGHEST, preferred_element_type=F32)
    return lax.dot_general(image, wide, NT, precision=HIGHEST, preferred_element_type=F32)


def first_kernel(blocks_ref, out_ref, own_ref, left, right, solved):
    gram = unpacked(blocks_ref[...])
    coefficients = reduce_gram(gram, left, right, solved)
    out_ref[...] = coefficients
    own_ref[...] = inner_of(coefficients, gram)


def merge_kernel(top_ref, upper_ref, out_ref, own_ref, left, right, solved):
    gram = whole_of(top_ref[...], upper_ref[...])
    coefficients = reduce_gram(gram, left, right, solved)
    out_ref[...] = coefficients
    own_ref[...] = inner_of(coefficients, gram)


def last_kernel(top_ref, upper_ref, stacked_ref, weighted_ref, basis_ref, merged_ref, left, right, solved):
    coefficients = reduce_gram(whole_of(top_ref[...], upper_ref[...]), left, right, solved)
    basis_ref[...] = combine(coefficients, stacked_ref[...])
    merged_ref[...] = combine(coefficients, weighted_ref[...])


def compress(kernel, outs, *operands):
    return pl.pallas_call(
        kernel,
        out_shape=outs,
        scratch_shapes=[pltpu.VMEM((RANK // PANEL, PANEL, TILE), F32)] * 3,
        compiler_params=pltpu.CompilerParams(vmem_limit_bytes=16 * 1024 * 1024),
        name="compress",
    )(*operands)


def combine(coefficients, rows):
    return jnp.dot(coefficients, rows, preferred_element_type=F32).astype(BF16)


def combine_two(coefficients, first, second):
    rows = first.shape[0]
    return (
        jnp.dot(coefficients[:, :rows], first, preferred_element_type=F32)
        + jnp.dot(coefficients[:, rows:], second, preferred_element_type=F32)
    ).astype(BF16)


def shared_out(rows, width, bit):
    pieces = [
        lax.dynamic_slice_in_dim(rows, (2 * pair + bit) * width, width, 1)
        for pair in range(rows.shape[1] // (2 * width))
    ]
    return pieces[0] if len(pieces) == 1 else jnp.concatenate(pieces, axis=1)


def ordered(upper_half, own_rows, partner_rows):
    lower_part = jnp.where(upper_half, partner_rows, own_rows)
    upper_part = jnp.where(upper_half, own_rows, partner_rows)
    return jnp.concatenate([lower_part, upper_part], axis=0)


def shards(snapshots, prior_basis, mass_factor, neighbours):
    weighted, gram = weigh(prior_basis, snapshots, mass_factor, neighbours)
    members = lax.axis_size("tm")
    places = members * lax.axis_size("space")
    across = [1 << i for i in range(members.bit_length() - 1, places.bit_length() - 1)]
    member = lax.axis_index("tm")
    width = snapshots.shape[1] // members
    partner_weighted = None
    reduced = (jax.ShapeDtypeStruct((RANK, 2 * RANK), BF16), jax.ShapeDtypeStruct((RANK, RANK), F32))
    coefficients, own = compress(first_kernel, reduced, total(gram, across, 1))
    for level in range(members.bit_length() - 1):
        step = 1 << level
        bit = member // step % 2
        upper_half = bit == 1
        partner_own = swapped(own, step)
        if partner_weighted is None:
            weighted = combine(coefficients, weighted)
            partner_weighted = swapped(shared_out(weighted, width, 1 - bit), step)
            own_weighted = shared_out(weighted, width, bit)
        else:
            partner_weighted = combine(swapped(coefficients, step), partner_weighted)
            own_weighted = combine(coefficients, shared_out(weighted, width, bit))
        weighted = ordered(upper_half, own_weighted, partner_weighted)
        if level == 0:
            stacked = combine_two(coefficients, prior_basis, snapshots)
        else:
            stacked = combine(coefficients, stacked)
        partner_stacked = swapped(shared_out(stacked, width, 1 - bit), step)
        stacked = ordered(upper_half, shared_out(stacked, width, bit), partner_stacked)
        top = lax.dot_general(weighted[:RANK], weighted, NT, preferred_element_type=F32)
        last = 2 * step == members
        if not last:
            next_bit = member // (2 * step) % 2
            partner_weighted = swapped(shared_out(weighted, width, 1 - next_bit), 2 * step)
        top = total(top, [1 << i for i in range(level + 1)] + across, 2)
        upper = jnp.where(upper_half, own, partner_own)
        if not last:
            coefficients, own = compress(merge_kernel, reduced, top, upper)
    share = jax.ShapeDtypeStruct((RANK, width), BF16)
    return compress(last_kernel, (share, share), top, upper, stacked, weighted)


def solution(mesh):
    return jax.shard_map(
        shards,
        mesh=mesh,
        in_specs=(P("tm", "space"), P("tm", "space"), P(None, None, "space"), P("space", None)),
        out_specs=(P(None, ("space", "tm")), P(None, ("space", "tm"))),
        check_vma=False,
    )
```

```python
import functools
import jax
import jax.numpy as jnp
from jax import lax
from jax.experimental import pallas as pl
from jax.experimental.pallas import tpu as pltpu
from jax.sharding import PartitionSpec as P

BLOCK_DOFS = 64
RANK = 64
REACH = 8
SUBSPACE_STEPS = 3
PANEL = 8
TILE = 128
F32 = jnp.float32
BF16 = jnp.bfloat16
HIGHEST = lax.Precision.HIGHEST
NT = (((1,), (1,)), ((), ()))


def halo(parts, axis, width):
    count = lax.axis_size(axis)
    forward = [(i, i + 1) for i in range(count - 1)]
    backward = [(target, source) for source, target in forward]
    last = jnp.concatenate([part[:, part.shape[1] - width:] for part in parts], axis=0)
    first = jnp.concatenate([part[:, :width] for part in parts], axis=0)
    low = lax.ppermute(last, axis, forward)
    high = lax.ppermute(first, axis, backward)
    return low, high


def swapped(block, mask):
    axes = ("space", "tm")
    count = lax.axis_size("space") * lax.axis_size("tm")
    return lax.ppermute(block, axes, [(i, i ^ mask) for i in range(count)])


def total(block, bits, stage):
    for start in range(0, len(bits), stage):
        first = bits[start]
        if stage == 2 and start + 1 < len(bits):
            second = bits[start + 1]
            near, far, both = swapped(block, first), swapped(block, second), swapped(block, first | second)
            block = (block + near) + (far + both)
        else:
            block = block + swapped(block, first)
    return block


def fill_odd(bank, whole, block, start, stop):
    bank[:, whole + start + TILE:whole + stop] = bank[:, start + block:stop - block]


def weigh_chunk(neighbours_ref, row, shift, bank, factor_ref):
    neighbours, block, chunk = factor_ref.shape
    columns = bank.shape[0]
    tiles = (bank.shape[1] - TILE) // (2 * TILE)
    lower = lax.broadcasted_iota(jnp.int32, (columns, TILE), 1) < block

    def spot_of(k, line):
        place = neighbours_ref[k, line] - shift
        odd = place & 1
        return (place >> 1) + (odd * (tiles + 1) if k % 2 == 0 else (1 - odd) * tiles)

    pieces = []
    for tile in range(chunk // TILE):
        results = []
        for side in range(2):
            parts = []
            for k in range(neighbours):
                spot = spot_of(k, row + tile * 2 + side)
                parts.append(bank[:, pl.ds(pl.multiple_of(spot * TILE, TILE), TILE)])
            joined = [jnp.where(lower, parts[k], parts[k + 1]) for k in range(0, neighbours - 1, 2)]
            if neighbours % 2:
                joined.append(parts[-1][:, :block])
            results.append(jnp.concatenate(joined, axis=1))
        left = jnp.concatenate(results, axis=0)
        right = factor_ref[:, :, tile * TILE:(tile + 1) * TILE].reshape(neighbours * block, TILE)
        product = jnp.dot(left, right, preferred_element_type=F32)
        pieces.append(jnp.where(lower, product[:columns], product[columns:]).astype(BF16))
    return jnp.concatenate(pieces, axis=1)


def inside_kernel(edge, spots, prior_ref, snap_ref, factor_ref, weighted_ref, gram_ref, bank):
    step = pl.program_id(0)
    rows, width = prior_ref.shape
    _, block, chunk = factor_ref.shape
    whole = width + 2 * edge

    @pl.when(step == 0)
    def _():
        bank[:rows, edge:edge + width] = prior_ref[...]
        bank[rows:, edge:edge + width] = snap_ref[...]
        fill_odd(bank, whole, block, edge, edge + width)
        gram_ref[...] = jnp.zeros_like(gram_ref)

    shift = lax.axis_index("space") * (width // block) - edge // block
    weighted = weigh_chunk(spots, (step + 1) * (chunk // block), shift, bank, factor_ref)
    weighted_ref[...] = weighted
    gram_ref[...] += lax.dot_general(weighted, weighted, NT, preferred_element_type=F32)


def packed(gram):
    half = gram.shape[0] // 2
    quarter = half // 2
    corner = gram[half:, half:]
    return jnp.concatenate([gram[:half], jnp.concatenate([corner[:quarter], corner[quarter:]], axis=1)], axis=0)


def unpacked(blocks):
    half = blocks.shape[1] // 2
    top, pair = blocks[:half], blocks[half:]
    corner = jnp.concatenate([pair[:, :half], pair[:, half:]], axis=0)
    return whole_of(top, corner)


def whole_of(top, corner):
    half = top.shape[0]
    return jnp.concatenate([top, jnp.concatenate([top.T[half:], corner], axis=1)], axis=0)


def border_kernel(
    width, spots, prior_ref, snap_ref, low_ref, high_ref, factor_ref, part_ref, kept_ref, weighted_ref, packed_ref, bank, gram
):
    step = pl.program_id(0)
    rows, span = prior_ref.shape
    edge = low_ref.shape[1]
    _, block, chunk = factor_ref.shape
    whole = span + edge

    @pl.when(step == 0)
    def _():
        bank[:, :edge] = low_ref[...]
        bank[:rows, edge:whole] = prior_ref[...]
        bank[rows:, edge:whole] = snap_ref[...]
        gram[...] = part_ref[...]

    @pl.when(step != 0)
    def _():
        bank[:rows, :span] = prior_ref[...]
        bank[rows:, :span] = snap_ref[...]
        bank[:, span:whole] = high_ref[...]

    fill_odd(bank, whole, block, 0, whole)
    bank[:, whole + block:whole + TILE] = bank[:, :block]
    bank[:, 2 * whole:2 * whole + block] = bank[:, whole - block:whole]
    shift = lax.axis_index("space") * (width // block) - edge // block + step * ((width + 2 * edge - whole) // block)
    weighted = weigh_chunk(spots, step * ((width - chunk) // block), shift, bank, factor_ref)
    weighted_ref[...] = weighted
    gram[...] += lax.dot_general(weighted, weighted, NT, preferred_element_type=F32)

    @pl.when(step == pl.num_programs(0) - 1)
    def _():
        packed_ref[...] = packed(gram[...])


def weigh(prior, snapshots, factor, neighbours):
    rows, width = prior.shape
    columns = 2 * rows
    count, block, _ = factor.shape
    edge = REACH * block
    chunk = 2 * edge
    span = 2 * chunk
    chunks = width // chunk
    low, high = halo((prior, snapshots), "space", edge)
    spots = neighbours.T
    full = lambda i, s: (0, 0)
    shapes = (
        jax.ShapeDtypeStruct((columns, width), BF16),
        jax.ShapeDtypeStruct((columns, columns), F32),
    )
    params = pltpu.CompilerParams(vmem_limit_bytes=24 * 1024 * 1024)
    weighted, gram = pl.pallas_call(
        functools.partial(inside_kernel, edge),
        out_shape=shapes,
        grid_spec=pltpu.PrefetchScalarGridSpec(
            num_scalar_prefetch=1,
            grid=(chunks - 2,),
            in_specs=[
                pl.BlockSpec((rows, width), full),
                pl.BlockSpec((rows, width), full),
                pl.BlockSpec((count, block, chunk), lambda i, s: (0, 0, i + 1)),
            ],
            out_specs=(
                pl.BlockSpec((columns, chunk), lambda i, s: (0, i + 1)),
                pl.BlockSpec((columns, columns), full),
            ),
            scratch_shapes=[pltpu.VMEM((columns, 2 * (width + 2 * edge) + TILE), BF16)],
        ),
        compiler_params=params,
        cost_estimate=pl.CostEstimate(
            flops=8 * columns * count * block * width, bytes_accessed=2 * factor.size, transcendentals=0
        ),
        name="weigh_inside",
    )(spots, prior, snapshots, factor)
    ends = width // span - 1
    return pl.pallas_call(
        functools.partial(border_kernel, width),
        out_shape=(shapes[0], jax.ShapeDtypeStruct((columns * 3 // 4, columns), F32)),
        grid_spec=pltpu.PrefetchScalarGridSpec(
            num_scalar_prefetch=1,
            grid=(2,),
            in_specs=[
                pl.BlockSpec((rows, span), lambda i, s: (0, i * ends)),
                pl.BlockSpec((rows, span), lambda i, s: (0, i * ends)),
                pl.BlockSpec((columns, edge), full),
                pl.BlockSpec((columns, edge), full),
                pl.BlockSpec((count, block, chunk), lambda i, s: (0, 0, i * (chunks - 1))),
                pl.BlockSpec((columns, columns), full),
                pl.BlockSpec(memory_space=pl.ANY),
            ],
            out_specs=(
                pl.BlockSpec((columns, chunk), lambda i, s: (0, i * (chunks - 1))),
                pl.BlockSpec((columns * 3 // 4, columns), full),
            ),
            scratch_shapes=[
                pltpu.VMEM((columns, 2 * (span + edge) + TILE), BF16),
                pltpu.VMEM((columns, columns), F32),
            ],
        ),
        input_output_aliases={7: 0},
        compiler_params=params,
        name="weigh_border",
    )(spots, prior, snapshots, low, high, factor, gram, weighted)


def lanes_of(group, column):
    return jnp.broadcast_to(group[:, column:column + 1], (group.shape[0], TILE))


def row_of(group, row):
    return jnp.broadcast_to(group[row:row + 1, :], group.shape)


def eliminate(left, right, solved):
    groups = left.shape[0]
    sub = lax.broadcasted_iota(jnp.int32, (PANEL, TILE), 0)

    for p in range(groups):
        pivot, image = left[p], right[p]
        cols = [lanes_of(pivot, PANEL * p + s) for s in range(PANEL)]
        d = [[row_of(cols[c], r) if r >= c else None for c in range(PANEL)] for r in range(PANEL)]
        rows_a = [row_of(pivot, r) for r in range(PANEL)]
        rows_n = [row_of(image, r) for r in range(PANEL)]
        inverse = []
        for s in range(PANEL):
            inverse.append(1.0 / d[s][s])
            for r in range(s + 1, PANEL):
                m = d[r][s] * inverse[s]
                for c in range(s + 1, r + 1):
                    d[r][c] = d[r][c] - m * d[c][s]
                rows_a[r] = rows_a[r] - m * rows_a[s]
                rows_n[r] = rows_n[r] - m * rows_n[s]
        for q in range(p + 1, groups):
            fresh_a, fresh_n = left[q], right[q]
            work = [lanes_of(fresh_a, PANEL * p + s) for s in range(PANEL)]
            for s in range(PANEL):
                factor = work[s] * inverse[s]
                for c in range(s + 1, PANEL):
                    work[c] = work[c] - factor * d[c][s]
                fresh_a = fresh_a - factor * rows_a[s]
                fresh_n = fresh_n - factor * rows_n[s]
            left[q] = fresh_a
            right[q] = fresh_n
        merged = rows_n[0] * lax.rsqrt(d[0][0])
        for r in range(1, PANEL):
            merged = jnp.where(sub == r, rows_n[r] * lax.rsqrt(d[r][r]), merged)
        solved[p] = merged


def reduce_gram(gram, left, right, solved):
    product = gram[:RANK]
    for _ in range(SUBSPACE_STEPS):
        image = jnp.dot(product, gram, precision=HIGHEST, preferred_element_type=F32)
        scale = 1.0 / jnp.sqrt(jnp.sum(product * image, axis=1, keepdims=True))
        normed = product * scale
        image = jnp.concatenate([image * scale, jnp.zeros((TILE - RANK, TILE), F32)], axis=0)
        inner = lax.dot_general(normed, image, NT, precision=HIGHEST, preferred_element_type=F32)
        left[...] = inner.reshape(left.shape)
        right[...] = normed.reshape(right.shape)
        eliminate(left, right, solved)
        weights = solved[...].reshape(RANK, TILE)
        product = jnp.dot(weights, gram, precision=HIGHEST, preferred_element_type=F32)
    lengths = jnp.sqrt(jnp.sum(product * product, axis=1, keepdims=True) + 1e-06)
    return (solved[...].reshape(RANK, TILE) * lengths).astype(BF16)


def inner_of(coefficients, gram):
    wide = coefficients.astype(F32)
    image = jnp.dot(wide, gram, precision=HIGHEST, preferred_element_type=F32)
    return lax.dot_general(image, wide, NT, precision=HIGHEST, preferred_element_type=F32)


def first_kernel(blocks_ref, out_ref, own_ref, left, right, solved):
    gram = unpacked(blocks_ref[...])
    coefficients = reduce_gram(gram, left, right, solved)
    out_ref[...] = coefficients
    own_ref[...] = inner_of(coefficients, gram)


def merge_kernel(top_ref, upper_ref, out_ref, own_ref, left, right, solved):
    gram = whole_of(top_ref[...], upper_ref[...])
    coefficients = reduce_gram(gram, left, right, solved)
    out_ref[...] = coefficients
    own_ref[...] = inner_of(coefficients, gram)


def last_kernel(top_ref, upper_ref, stacked_ref, weighted_ref, basis_ref, merged_ref, left, right, solved):
    coefficients = reduce_gram(whole_of(top_ref[...], upper_ref[...]), left, right, solved)
    basis_ref[...] = combine(coefficients, stacked_ref[...])
    merged_ref[...] = combine(coefficients, weighted_ref[...])


def compress(kernel, outs, *operands):
    return pl.pallas_call(
        kernel,
        out_shape=outs,
        scratch_shapes=[pltpu.VMEM((RANK // PANEL, PANEL, TILE), F32)] * 3,
        compiler_params=pltpu.CompilerParams(vmem_limit_bytes=16 * 1024 * 1024),
        name="compress",
    )(*operands)


def combine(coefficients, rows):
    return jnp.dot(coefficients, rows, preferred_element_type=F32).astype(BF16)


def combine_two(coefficients, first, second):
    rows = first.shape[0]
    return (
        jnp.dot(coefficients[:, :rows], first, preferred_element_type=F32)
        + jnp.dot(coefficients[:, rows:], second, preferred_element_type=F32)
    ).astype(BF16)


def shared_out(rows, width, bit):
    pieces = [
        lax.dynamic_slice_in_dim(rows, (2 * pair + bit) * width, width, 1)
        for pair in range(rows.shape[1] // (2 * width))
    ]
    return pieces[0] if len(pieces) == 1 else jnp.concatenate(pieces, axis=1)


def ordered(upper_half, own_rows, partner_rows):
    lower_part = jnp.where(upper_half, partner_rows, own_rows)
    upper_part = jnp.where(upper_half, own_rows, partner_rows)
    return jnp.concatenate([lower_part, upper_part], axis=0)


def shards(snapshots, prior_basis, mass_factor, neighbours):
    weighted, gram = weigh(prior_basis, snapshots, mass_factor, neighbours)
    members = lax.axis_size("tm")
    places = members * lax.axis_size("space")
    across = [1 << i for i in range(members.bit_length() - 1, places.bit_length() - 1)]
    member = lax.axis_index("tm")
    width = snapshots.shape[1] // members
    partner_weighted = None
    reduced = (jax.ShapeDtypeStruct((RANK, 2 * RANK), BF16), jax.ShapeDtypeStruct((RANK, RANK), F32))
    coefficients, own = compress(first_kernel, reduced, total(gram, across, 1))
    for level in range(members.bit_length() - 1):
        step = 1 << level
        bit = member // step % 2
        upper_half = bit == 1
        if partner_weighted is None:
            weighted = combine(coefficients, weighted)
            partner_weighted = swapped(shared_out(weighted, width, 1 - bit), step)
            own_weighted = shared_out(weighted, width, bit)
        else:
            partner_weighted = combine(swapped(coefficients, step), partner_weighted)
            own_weighted = combine(coefficients, shared_out(weighted, width, bit))
        weighted = ordered(upper_half, own_weighted, partner_weighted)
        top = lax.dot_general(weighted[:RANK], weighted, NT, preferred_element_type=F32)
        last = 2 * step == members
        if not last:
            next_bit = member // (2 * step) % 2
            partner_weighted = swapped(shared_out(weighted, width, 1 - next_bit), 2 * step)
        bits = [1 << i for i in range(level + 1)] + across
        top = total(top, bits[:2], 2)
        coefficients, own, top = lax.optimization_barrier((coefficients, own, top))
        partner_own = swapped(own, step)
        if level == 0:
            stacked = combine_two(coefficients, prior_basis, snapshots)
        else:
            stacked = combine(coefficients, stacked)
        partner_stacked = swapped(shared_out(stacked, width, 1 - bit), step)
        stacked = ordered(upper_half, shared_out(stacked, width, bit), partner_stacked)
        top = total(top, bits[2:], 2)
        upper = jnp.where(upper_half, own, partner_own)
        if not last:
            coefficients, own = compress(merge_kernel, reduced, top, upper)
    share = jax.ShapeDtypeStruct((RANK, width), BF16)
    return compress(last_kernel, (share, share), top, upper, stacked, weighted)


def solution(mesh):
    return jax.shard_map(
        shards,
        mesh=mesh,
        in_specs=(P("tm", "space"), P("tm", "space"), P(None, None, "space"), P("space", None)),
        out_specs=(P(None, ("space", "tm")), P(None, ("space", "tm"))),
        check_vma=False,
    )
```

```python
import functools
import jax
import jax.numpy as jnp
from jax import lax
from jax.experimental import pallas as pl
from jax.experimental.pallas import tpu as pltpu
from jax.sharding import PartitionSpec as P

BLOCK_DOFS = 64
RANK = 64
REACH = 8
SUBSPACE_STEPS = 3
PANEL = 8
TILE = 128
F32 = jnp.float32
BF16 = jnp.bfloat16
HIGHEST = lax.Precision.HIGHEST
NT = (((1,), (1,)), ((), ()))


def halo(parts, axis, width):
    count = lax.axis_size(axis)
    forward = [(i, i + 1) for i in range(count - 1)]
    backward = [(target, source) for source, target in forward]
    last = jnp.concatenate([part[:, part.shape[1] - width:] for part in parts], axis=0)
    first = jnp.concatenate([part[:, :width] for part in parts], axis=0)
    low = lax.ppermute(last, axis, forward)
    high = lax.ppermute(first, axis, backward)
    return low, high


def swapped(block, mask):
    axes = ("space", "tm")
    count = lax.axis_size("space") * lax.axis_size("tm")
    return lax.ppermute(block, axes, [(i, i ^ mask) for i in range(count)])


def total(block, bits, stage):
    for start in range(0, len(bits), stage):
        first = bits[start]
        if stage == 2 and start + 1 < len(bits):
            second = bits[start + 1]
            near, far, both = swapped(block, first), swapped(block, second), swapped(block, first | second)
            block = (block + near) + (far + both)
        else:
            block = block + swapped(block, first)
    return block


def fill_odd(bank, whole, block, start, stop):
    bank[:, whole + start + TILE:whole + stop] = bank[:, start + block:stop - block]


def weigh_chunk(neighbours_ref, row, shift, bank, factor_ref):
    neighbours, block, chunk = factor_ref.shape
    columns = bank.shape[0]
    tiles = (bank.shape[1] - TILE) // (2 * TILE)
    lower = lax.broadcasted_iota(jnp.int32, (columns, TILE), 1) < block

    def spot_of(k, line):
        place = neighbours_ref[k, line] - shift
        odd = place & 1
        return (place >> 1) + (odd * (tiles + 1) if k % 2 == 0 else (1 - odd) * tiles)

    pieces = []
    for tile in range(chunk // TILE):
        results = []
        for side in range(2):
            parts = []
            for k in range(neighbours):
                spot = spot_of(k, row + tile * 2 + side)
                parts.append(bank[:, pl.ds(pl.multiple_of(spot * TILE, TILE), TILE)])
            joined = [jnp.where(lower, parts[k], parts[k + 1]) for k in range(0, neighbours - 1, 2)]
            if neighbours % 2:
                joined.append(parts[-1][:, :block])
            results.append(jnp.concatenate(joined, axis=1))
        left = jnp.concatenate(results, axis=0)
        right = factor_ref[:, :, tile * TILE:(tile + 1) * TILE].reshape(neighbours * block, TILE)
        product = jnp.dot(left, right, preferred_element_type=F32)
        pieces.append(jnp.where(lower, product[:columns], product[columns:]).astype(BF16))
    return jnp.concatenate(pieces, axis=1)


def inside_kernel(edge, spots, prior_ref, snap_ref, factor_ref, weighted_ref, gram_ref, bank):
    step = pl.program_id(0)
    rows, width = prior_ref.shape
    _, block, chunk = factor_ref.shape
    whole = width + 2 * edge

    @pl.when(step == 0)
    def _():
        bank[:rows, edge:edge + width] = prior_ref[...]
        bank[rows:, edge:edge + width] = snap_ref[...]
        fill_odd(bank, whole, block, edge, edge + width)
        gram_ref[...] = jnp.zeros_like(gram_ref)

    shift = lax.axis_index("space") * (width // block) - edge // block
    weighted = weigh_chunk(spots, (step + 1) * (chunk // block), shift, bank, factor_ref)
    weighted_ref[...] = weighted
    gram_ref[...] += lax.dot_general(weighted, weighted, NT, preferred_element_type=F32)


def packed(gram):
    half = gram.shape[0] // 2
    quarter = half // 2
    corner = gram[half:, half:]
    return jnp.concatenate([gram[:half], jnp.concatenate([corner[:quarter], corner[quarter:]], axis=1)], axis=0)


def unpacked(blocks):
    half = blocks.shape[1] // 2
    top, pair = blocks[:half], blocks[half:]
    corner = jnp.concatenate([pair[:, :half], pair[:, half:]], axis=0)
    return whole_of(top, corner)


def whole_of(top, corner):
    half = top.shape[0]
    return jnp.concatenate([top, jnp.concatenate([top.T[half:], corner], axis=1)], axis=0)


def border_kernel(
    width, spots, prior_ref, snap_ref, low_ref, high_ref, factor_ref, part_ref, kept_ref, weighted_ref, packed_ref, bank, gram
):
    step = pl.program_id(0)
    rows, span = prior_ref.shape
    edge = low_ref.shape[1]
    _, block, chunk = factor_ref.shape
    whole = span + edge

    @pl.when(step == 0)
    def _():
        bank[:, :edge] = low_ref[...]
        bank[:rows, edge:whole] = prior_ref[...]
        bank[rows:, edge:whole] = snap_ref[...]
        gram[...] = part_ref[...]

    @pl.when(step != 0)
    def _():
        bank[:rows, :span] = prior_ref[...]
        bank[rows:, :span] = snap_ref[...]
        bank[:, span:whole] = high_ref[...]

    fill_odd(bank, whole, block, 0, whole)
    bank[:, whole + block:whole + TILE] = bank[:, :block]
    bank[:, 2 * whole:2 * whole + block] = bank[:, whole - block:whole]
    shift = lax.axis_index("space") * (width // block) - edge // block + step * ((width + 2 * edge - whole) // block)
    weighted = weigh_chunk(spots, step * ((width - chunk) // block), shift, bank, factor_ref)
    weighted_ref[...] = weighted
    gram[...] += lax.dot_general(weighted, weighted, NT, preferred_element_type=F32)

    @pl.when(step == pl.num_programs(0) - 1)
    def _():
        packed_ref[...] = packed(gram[...])


def weigh(prior, snapshots, factor, neighbours):
    rows, width = prior.shape
    columns = 2 * rows
    count, block, _ = factor.shape
    edge = REACH * block
    chunk = 2 * edge
    span = 2 * chunk
    chunks = width // chunk
    low, high = halo((prior, snapshots), "space", edge)
    spots = neighbours.T
    full = lambda i, s: (0, 0)
    shapes = (
        jax.ShapeDtypeStruct((columns, width), BF16),
        jax.ShapeDtypeStruct((columns, columns), F32),
    )
    params = pltpu.CompilerParams(vmem_limit_bytes=24 * 1024 * 1024)
    weighted, gram = pl.pallas_call(
        functools.partial(inside_kernel, edge),
        out_shape=shapes,
        grid_spec=pltpu.PrefetchScalarGridSpec(
            num_scalar_prefetch=1,
            grid=(chunks - 2,),
            in_specs=[
                pl.BlockSpec((rows, width), full),
                pl.BlockSpec((rows, width), full),
                pl.BlockSpec((count, block, chunk), lambda i, s: (0, 0, i + 1)),
            ],
            out_specs=(
                pl.BlockSpec((columns, chunk), lambda i, s: (0, i + 1)),
                pl.BlockSpec((columns, columns), full),
            ),
            scratch_shapes=[pltpu.VMEM((columns, 2 * (width + 2 * edge) + TILE), BF16)],
        ),
        compiler_params=params,
        cost_estimate=pl.CostEstimate(
            flops=8 * columns * count * block * width, bytes_accessed=2 * factor.size, transcendentals=0
        ),
        name="weigh_inside",
    )(spots, prior, snapshots, factor)
    ends = width // span - 1
    return pl.pallas_call(
        functools.partial(border_kernel, width),
        out_shape=(shapes[0], jax.ShapeDtypeStruct((columns * 3 // 4, columns), F32)),
        grid_spec=pltpu.PrefetchScalarGridSpec(
            num_scalar_prefetch=1,
            grid=(2,),
            in_specs=[
                pl.BlockSpec((rows, span), lambda i, s: (0, i * ends)),
                pl.BlockSpec((rows, span), lambda i, s: (0, i * ends)),
                pl.BlockSpec((columns, edge), full),
                pl.BlockSpec((columns, edge), full),
                pl.BlockSpec((count, block, chunk), lambda i, s: (0, 0, i * (chunks - 1))),
                pl.BlockSpec((columns, columns), full),
                pl.BlockSpec(memory_space=pl.ANY),
            ],
            out_specs=(
                pl.BlockSpec((columns, chunk), lambda i, s: (0, i * (chunks - 1))),
                pl.BlockSpec((columns * 3 // 4, columns), full),
            ),
            scratch_shapes=[
                pltpu.VMEM((columns, 2 * (span + edge) + TILE), BF16),
                pltpu.VMEM((columns, columns), F32),
            ],
        ),
        input_output_aliases={7: 0},
        compiler_params=params,
        name="weigh_border",
    )(spots, prior, snapshots, low, high, factor, gram, weighted)


def lanes_of(group, column):
    return jnp.broadcast_to(group[:, column:column + 1], (group.shape[0], TILE))


def row_of(group, row):
    return jnp.broadcast_to(group[row:row + 1, :], group.shape)


def eliminate(left, right, solved):
    groups = left.shape[0]
    sub = lax.broadcasted_iota(jnp.int32, (PANEL, TILE), 0)

    for p in range(groups):
        pivot, image = left[p], right[p]
        cols = [lanes_of(pivot, PANEL * p + s) for s in range(PANEL)]
        d = [[row_of(cols[c], r) if r >= c else None for c in range(PANEL)] for r in range(PANEL)]
        rows_a = [row_of(pivot, r) for r in range(PANEL)]
        rows_n = [row_of(image, r) for r in range(PANEL)]
        inverse = []
        for s in range(PANEL):
            inverse.append(1.0 / d[s][s])
            for r in range(s + 1, PANEL):
                m = d[r][s] * inverse[s]
                for c in range(s + 1, r + 1):
                    d[r][c] = d[r][c] - m * d[c][s]
                rows_a[r] = rows_a[r] - m * rows_a[s]
                rows_n[r] = rows_n[r] - m * rows_n[s]
        for q in range(p + 1, groups):
            fresh_a, fresh_n = left[q], right[q]
            work = [lanes_of(fresh_a, PANEL * p + s) for s in range(PANEL)]
            for s in range(PANEL):
                factor = work[s] * inverse[s]
                for c in range(s + 1, PANEL):
                    work[c] = work[c] - factor * d[c][s]
                fresh_a = fresh_a - factor * rows_a[s]
                fresh_n = fresh_n - factor * rows_n[s]
            left[q] = fresh_a
            right[q] = fresh_n
        merged = rows_n[0] * lax.rsqrt(d[0][0])
        for r in range(1, PANEL):
            merged = jnp.where(sub == r, rows_n[r] * lax.rsqrt(d[r][r]), merged)
        solved[p] = merged


def reduce_gram(gram, left, right, solved):
    product = gram[:RANK]
    for _ in range(SUBSPACE_STEPS):
        image = jnp.dot(product, gram, precision=HIGHEST, preferred_element_type=F32)
        scale = 1.0 / jnp.sqrt(jnp.sum(product * image, axis=1, keepdims=True))
        normed = product * scale
        image = jnp.concatenate([image * scale, jnp.zeros((TILE - RANK, TILE), F32)], axis=0)
        inner = lax.dot_general(normed, image, NT, precision=HIGHEST, preferred_element_type=F32)
        left[...] = inner.reshape(left.shape)
        right[...] = normed.reshape(right.shape)
        eliminate(left, right, solved)
        weights = solved[...].reshape(RANK, TILE)
        product = jnp.dot(weights, gram, precision=HIGHEST, preferred_element_type=F32)
    lengths = jnp.sqrt(jnp.sum(product * product, axis=1, keepdims=True) + 1e-06)
    return (solved[...].reshape(RANK, TILE) * lengths).astype(BF16)


def inner_of(coefficients, gram):
    wide = coefficients.astype(F32)
    image = jnp.dot(wide, gram, precision=HIGHEST, preferred_element_type=F32)
    return lax.dot_general(image, wide, NT, precision=HIGHEST, preferred_element_type=F32)


def first_kernel(blocks_ref, out_ref, own_ref, left, right, solved):
    gram = unpacked(blocks_ref[...])
    coefficients = reduce_gram(gram, left, right, solved)
    out_ref[...] = coefficients
    own_ref[...] = inner_of(coefficients, gram)


def merge_kernel(top_ref, upper_ref, out_ref, own_ref, left, right, solved):
    gram = whole_of(top_ref[...], upper_ref[...])
    coefficients = reduce_gram(gram, left, right, solved)
    out_ref[...] = coefficients
    own_ref[...] = inner_of(coefficients, gram)


def last_kernel(top_ref, upper_ref, stacked_ref, weighted_ref, basis_ref, merged_ref, left, right, solved):
    coefficients = reduce_gram(whole_of(top_ref[...], upper_ref[...]), left, right, solved)
    basis_ref[...] = combine(coefficients, stacked_ref[...])
    merged_ref[...] = combine(coefficients, weighted_ref[...])


def compress(kernel, outs, *operands):
    return pl.pallas_call(
        kernel,
        out_shape=outs,
        scratch_shapes=[pltpu.VMEM((RANK // PANEL, PANEL, TILE), F32)] * 3,
        compiler_params=pltpu.CompilerParams(vmem_limit_bytes=16 * 1024 * 1024),
        name="compress",
    )(*operands)


def combine(coefficients, rows):
    return jnp.dot(coefficients, rows, preferred_element_type=F32).astype(BF16)


def combine_two(coefficients, first, second):
    rows = first.shape[0]
    return (
        jnp.dot(coefficients[:, :rows], first, preferred_element_type=F32)
        + jnp.dot(coefficients[:, rows:], second, preferred_element_type=F32)
    ).astype(BF16)


def shared_out(rows, width, bit):
    pieces = [
        lax.dynamic_slice_in_dim(rows, (2 * pair + bit) * width, width, 1)
        for pair in range(rows.shape[1] // (2 * width))
    ]
    return pieces[0] if len(pieces) == 1 else jnp.concatenate(pieces, axis=1)


def ordered(upper_half, own_rows, partner_rows):
    lower_part = jnp.where(upper_half, partner_rows, own_rows)
    upper_part = jnp.where(upper_half, own_rows, partner_rows)
    return jnp.concatenate([lower_part, upper_part], axis=0)


def shards(snapshots, prior_basis, mass_factor, neighbours):
    weighted, gram = weigh(prior_basis, snapshots, mass_factor, neighbours)
    members = lax.axis_size("tm")
    places = members * lax.axis_size("space")
    across = [1 << i for i in range(members.bit_length() - 1, places.bit_length() - 1)]
    member = lax.axis_index("tm")
    width = snapshots.shape[1] // members
    partner_weighted = None
    reduced = (jax.ShapeDtypeStruct((RANK, 2 * RANK), BF16), jax.ShapeDtypeStruct((RANK, RANK), F32))
    coefficients, own = compress(first_kernel, reduced, total(gram, across, 1))
    for level in range(members.bit_length() - 1):
        step = 1 << level
        bit = member // step % 2
        upper_half = bit == 1
        if partner_weighted is None:
            weighted = combine(coefficients, weighted)
            partner_weighted = swapped(shared_out(weighted, width, 1 - bit), step)
            own_weighted = shared_out(weighted, width, bit)
        else:
            partner_weighted = combine(swapped(coefficients, step), partner_weighted)
            own_weighted = combine(coefficients, shared_out(weighted, width, bit))
        weighted = ordered(upper_half, own_weighted, partner_weighted)
        top = lax.dot_general(weighted[:RANK], weighted, NT, preferred_element_type=F32)
        last = 2 * step == members
        bits = [1 << i for i in range(level + 1)] + across
        top = total(top, bits[:2], 2)
        coefficients, own, weighted, top = lax.optimization_barrier((coefficients, own, weighted, top))
        if not last:
            next_bit = member // (2 * step) % 2
            partner_weighted = swapped(shared_out(weighted, width, 1 - next_bit), 2 * step)
        partner_own = swapped(own, step)
        if level == 0:
            stacked = combine_two(coefficients, prior_basis, snapshots)
        else:
            stacked = combine(coefficients, stacked)
        partner_stacked = swapped(shared_out(stacked, width, 1 - bit), step)
        stacked = ordered(upper_half, shared_out(stacked, width, bit), partner_stacked)
        top = total(top, bits[2:], 2)
        upper = jnp.where(upper_half, own, partner_own)
        if not last:
            coefficients, own = compress(merge_kernel, reduced, top, upper)
    share = jax.ShapeDtypeStruct((RANK, width), BF16)
    return compress(last_kernel, (share, share), top, upper, stacked, weighted)


def solution(mesh):
    return jax.shard_map(
        shards,
        mesh=mesh,
        in_specs=(P("tm", "space"), P("tm", "space"), P(None, None, "space"), P("space", None)),
        out_specs=(P(None, ("space", "tm")), P(None, ("space", "tm"))),
        check_vma=False,
    )
```

```python
import functools
import jax
import jax.numpy as jnp
from jax import lax
from jax.experimental import pallas as pl
from jax.experimental.pallas import tpu as pltpu
from jax.sharding import PartitionSpec as P

BLOCK_DOFS = 64
RANK = 64
REACH = 8
SUBSPACE_STEPS = 3
PANEL = 8
TILE = 128
F32 = jnp.float32
BF16 = jnp.bfloat16
HIGHEST = lax.Precision.HIGHEST
NT = (((1,), (1,)), ((), ()))


def halo(parts, axis, width):
    count = lax.axis_size(axis)
    forward = [(i, i + 1) for i in range(count - 1)]
    backward = [(target, source) for source, target in forward]
    last = jnp.concatenate([part[:, part.shape[1] - width:] for part in parts], axis=0)
    first = jnp.concatenate([part[:, :width] for part in parts], axis=0)
    low = lax.ppermute(last, axis, forward)
    high = lax.ppermute(first, axis, backward)
    return low, high


def swapped(block, mask):
    axes = ("space", "tm")
    count = lax.axis_size("space") * lax.axis_size("tm")
    return lax.ppermute(block, axes, [(i, i ^ mask) for i in range(count)])


def total(block, bits, stage):
    for start in range(0, len(bits), stage):
        first = bits[start]
        if stage == 2 and start + 1 < len(bits):
            second = bits[start + 1]
            near, far, both = swapped(block, first), swapped(block, second), swapped(block, first | second)
            block = (block + near) + (far + both)
        else:
            block = block + swapped(block, first)
    return block


def fill_odd(bank, whole, block, start, stop):
    bank[:, whole + start + TILE:whole + stop] = bank[:, start + block:stop - block]


def weigh_chunk(neighbours_ref, row, shift, bank, factor_ref):
    neighbours, block, chunk = factor_ref.shape
    columns = bank.shape[0]
    tiles = (bank.shape[1] - TILE) // (2 * TILE)
    lower = lax.broadcasted_iota(jnp.int32, (columns, TILE), 1) < block

    def spot_of(k, line):
        place = neighbours_ref[k, line] - shift
        odd = place & 1
        return (place >> 1) + (odd * (tiles + 1) if k % 2 == 0 else (1 - odd) * tiles)

    pieces = []
    for tile in range(chunk // TILE):
        results = []
        for side in range(2):
            parts = []
            for k in range(neighbours):
                spot = spot_of(k, row + tile * 2 + side)
                parts.append(bank[:, pl.ds(pl.multiple_of(spot * TILE, TILE), TILE)])
            joined = [jnp.where(lower, parts[k], parts[k + 1]) for k in range(0, neighbours - 1, 2)]
            if neighbours % 2:
                joined.append(parts[-1][:, :block])
            results.append(jnp.concatenate(joined, axis=1))
        left = jnp.concatenate(results, axis=0)
        right = factor_ref[:, :, tile * TILE:(tile + 1) * TILE].reshape(neighbours * block, TILE)
        product = jnp.dot(left, right, preferred_element_type=F32)
        pieces.append(jnp.where(lower, product[:columns], product[columns:]).astype(BF16))
    return jnp.concatenate(pieces, axis=1)


def inside_kernel(edge, spots, prior_ref, snap_ref, factor_ref, weighted_ref, gram_ref, bank):
    step = pl.program_id(0)
    rows, width = prior_ref.shape
    _, block, chunk = factor_ref.shape
    whole = width + 2 * edge

    @pl.when(step == 0)
    def _():
        bank[:rows, edge:edge + width] = prior_ref[...]
        bank[rows:, edge:edge + width] = snap_ref[...]
        fill_odd(bank, whole, block, edge, edge + width)
        gram_ref[...] = jnp.zeros_like(gram_ref)

    shift = lax.axis_index("space") * (width // block) - edge // block
    weighted = weigh_chunk(spots, (step + 1) * (chunk // block), shift, bank, factor_ref)
    weighted_ref[...] = weighted
    gram_ref[...] += lax.dot_general(weighted, weighted, NT, preferred_element_type=F32)


def packed(gram):
    half = gram.shape[0] // 2
    quarter = half // 2
    corner = gram[half:, half:]
    return jnp.concatenate([gram[:half], jnp.concatenate([corner[:quarter], corner[quarter:]], axis=1)], axis=0)


def unpacked(blocks):
    half = blocks.shape[1] // 2
    top, pair = blocks[:half], blocks[half:]
    corner = jnp.concatenate([pair[:, :half], pair[:, half:]], axis=0)
    return whole_of(top, corner)


def whole_of(top, corner):
    half = top.shape[0]
    return jnp.concatenate([top, jnp.concatenate([top.T[half:], corner], axis=1)], axis=0)


def border_kernel(
    width, spots, prior_ref, snap_ref, low_ref, high_ref, factor_ref, part_ref, kept_ref, weighted_ref, packed_ref, bank, gram
):
    step = pl.program_id(0)
    rows, span = prior_ref.shape
    edge = low_ref.shape[1]
    _, block, chunk = factor_ref.shape
    whole = span + edge

    @pl.when(step == 0)
    def _():
        bank[:, :edge] = low_ref[...]
        bank[:rows, edge:whole] = prior_ref[...]
        bank[rows:, edge:whole] = snap_ref[...]
        gram[...] = part_ref[...]

    @pl.when(step != 0)
    def _():
        bank[:rows, :span] = prior_ref[...]
        bank[rows:, :span] = snap_ref[...]
        bank[:, span:whole] = high_ref[...]

    fill_odd(bank, whole, block, 0, whole)
    bank[:, whole + block:whole + TILE] = bank[:, :block]
    bank[:, 2 * whole:2 * whole + block] = bank[:, whole - block:whole]
    shift = lax.axis_index("space") * (width // block) - edge // block + step * ((width + 2 * edge - whole) // block)
    weighted = weigh_chunk(spots, step * ((width - chunk) // block), shift, bank, factor_ref)
    weighted_ref[...] = weighted
    gram[...] += lax.dot_general(weighted, weighted, NT, preferred_element_type=F32)

    @pl.when(step == pl.num_programs(0) - 1)
    def _():
        packed_ref[...] = packed(gram[...])


def weigh(prior, snapshots, factor, neighbours):
    rows, width = prior.shape
    columns = 2 * rows
    count, block, _ = factor.shape
    edge = REACH * block
    chunk = 2 * edge
    span = 2 * chunk
    chunks = width // chunk
    low, high = halo((prior, snapshots), "space", edge)
    spots = neighbours.T
    full = lambda i, s: (0, 0)
    shapes = (
        jax.ShapeDtypeStruct((columns, width), BF16),
        jax.ShapeDtypeStruct((columns, columns), F32),
    )
    params = pltpu.CompilerParams(vmem_limit_bytes=24 * 1024 * 1024)
    weighted, gram = pl.pallas_call(
        functools.partial(inside_kernel, edge),
        out_shape=shapes,
        grid_spec=pltpu.PrefetchScalarGridSpec(
            num_scalar_prefetch=1,
            grid=(chunks - 2,),
            in_specs=[
                pl.BlockSpec((rows, width), full),
                pl.BlockSpec((rows, width), full),
                pl.BlockSpec((count, block, chunk), lambda i, s: (0, 0, i + 1)),
            ],
            out_specs=(
                pl.BlockSpec((columns, chunk), lambda i, s: (0, i + 1)),
                pl.BlockSpec((columns, columns), full),
            ),
            scratch_shapes=[pltpu.VMEM((columns, 2 * (width + 2 * edge) + TILE), BF16)],
        ),
        compiler_params=params,
        cost_estimate=pl.CostEstimate(
            flops=8 * columns * count * block * width, bytes_accessed=2 * factor.size, transcendentals=0
        ),
        name="weigh_inside",
    )(spots, prior, snapshots, factor)
    ends = width // span - 1
    return pl.pallas_call(
        functools.partial(border_kernel, width),
        out_shape=(shapes[0], jax.ShapeDtypeStruct((columns * 3 // 4, columns), F32)),
        grid_spec=pltpu.PrefetchScalarGridSpec(
            num_scalar_prefetch=1,
            grid=(2,),
            in_specs=[
                pl.BlockSpec((rows, span), lambda i, s: (0, i * ends)),
                pl.BlockSpec((rows, span), lambda i, s: (0, i * ends)),
                pl.BlockSpec((columns, edge), full),
                pl.BlockSpec((columns, edge), full),
                pl.BlockSpec((count, block, chunk), lambda i, s: (0, 0, i * (chunks - 1))),
                pl.BlockSpec((columns, columns), full),
                pl.BlockSpec(memory_space=pl.ANY),
            ],
            out_specs=(
                pl.BlockSpec((columns, chunk), lambda i, s: (0, i * (chunks - 1))),
                pl.BlockSpec((columns * 3 // 4, columns), full),
            ),
            scratch_shapes=[
                pltpu.VMEM((columns, 2 * (span + edge) + TILE), BF16),
                pltpu.VMEM((columns, columns), F32),
            ],
        ),
        input_output_aliases={7: 0},
        compiler_params=params,
        name="weigh_border",
    )(spots, prior, snapshots, low, high, factor, gram, weighted)


def lanes_of(group, column):
    return jnp.broadcast_to(group[:, column:column + 1], (group.shape[0], TILE))


def row_of(group, row):
    return jnp.broadcast_to(group[row:row + 1, :], group.shape)


def eliminate(left, right, solved):
    groups = left.shape[0]
    sub = lax.broadcasted_iota(jnp.int32, (PANEL, TILE), 0)

    for p in range(groups):
        pivot, image = left[p], right[p]
        cols = [lanes_of(pivot, PANEL * p + s) for s in range(PANEL)]
        d = [[row_of(cols[c], r) if r >= c else None for c in range(PANEL)] for r in range(PANEL)]
        rows_a = [row_of(pivot, r) for r in range(PANEL)]
        rows_n = [row_of(image, r) for r in range(PANEL)]
        inverse = []
        for s in range(PANEL):
            inverse.append(1.0 / d[s][s])
            for r in range(s + 1, PANEL):
                m = d[r][s] * inverse[s]
                for c in range(s + 1, r + 1):
                    d[r][c] = d[r][c] - m * d[c][s]
                rows_a[r] = rows_a[r] - m * rows_a[s]
                rows_n[r] = rows_n[r] - m * rows_n[s]
        for q in range(p + 1, groups):
            fresh_a, fresh_n = left[q], right[q]
            work = [lanes_of(fresh_a, PANEL * p + s) for s in range(PANEL)]
            for s in range(PANEL):
                factor = work[s] * inverse[s]
                for c in range(s + 1, PANEL):
                    work[c] = work[c] - factor * d[c][s]
                fresh_a = fresh_a - factor * rows_a[s]
                fresh_n = fresh_n - factor * rows_n[s]
            left[q] = fresh_a
            right[q] = fresh_n
        merged = rows_n[0] * lax.rsqrt(d[0][0])
        for r in range(1, PANEL):
            merged = jnp.where(sub == r, rows_n[r] * lax.rsqrt(d[r][r]), merged)
        solved[p] = merged


def reduce_gram(gram, left, right, solved):
    product = gram[:RANK]
    for _ in range(SUBSPACE_STEPS):
        image = jnp.dot(product, gram, precision=HIGHEST, preferred_element_type=F32)
        scale = 1.0 / jnp.sqrt(jnp.sum(product * image, axis=1, keepdims=True))
        normed = product * scale
        image = jnp.concatenate([image * scale, jnp.zeros((TILE - RANK, TILE), F32)], axis=0)
        inner = lax.dot_general(normed, image, NT, precision=HIGHEST, preferred_element_type=F32)
        left[...] = inner.reshape(left.shape)
        right[...] = normed.reshape(right.shape)
        eliminate(left, right, solved)
        weights = solved[...].reshape(RANK, TILE)
        product = jnp.dot(weights, gram, precision=HIGHEST, preferred_element_type=F32)
    lengths = jnp.sqrt(jnp.sum(product * product, axis=1, keepdims=True) + 1e-06)
    return (solved[...].reshape(RANK, TILE) * lengths).astype(BF16)


def inner_of(coefficients, gram):
    wide = coefficients.astype(F32)
    image = jnp.dot(wide, gram, precision=HIGHEST, preferred_element_type=F32)
    return lax.dot_general(image, wide, NT, precision=HIGHEST, preferred_element_type=F32)


def first_kernel(blocks_ref, out_ref, own_ref, left, right, solved):
    gram = unpacked(blocks_ref[...])
    coefficients = reduce_gram(gram, left, right, solved)
    out_ref[...] = coefficients
    own_ref[...] = inner_of(coefficients, gram)


def merge_kernel(top_ref, upper_ref, out_ref, own_ref, left, right, solved):
    gram = whole_of(top_ref[...], upper_ref[...])
    coefficients = reduce_gram(gram, left, right, solved)
    out_ref[...] = coefficients
    own_ref[...] = inner_of(coefficients, gram)


def last_kernel(top_ref, upper_ref, stacked_ref, weighted_ref, basis_ref, merged_ref, left, right, solved):
    coefficients = reduce_gram(whole_of(top_ref[...], upper_ref[...]), left, right, solved)
    basis_ref[...] = combine(coefficients, stacked_ref[...])
    merged_ref[...] = combine(coefficients, weighted_ref[...])


def compress(kernel, outs, *operands):
    return pl.pallas_call(
        kernel,
        out_shape=outs,
        scratch_shapes=[pltpu.VMEM((RANK // PANEL, PANEL, TILE), F32)] * 3,
        compiler_params=pltpu.CompilerParams(vmem_limit_bytes=16 * 1024 * 1024),
        name="compress",
    )(*operands)


def combine(coefficients, rows):
    return jnp.dot(coefficients, rows, preferred_element_type=F32).astype(BF16)


def combine_two(coefficients, first, second):
    rows = first.shape[0]
    return (
        jnp.dot(coefficients[:, :rows], first, preferred_element_type=F32)
        + jnp.dot(coefficients[:, rows:], second, preferred_element_type=F32)
    ).astype(BF16)


def shared_out(rows, width, bit):
    pieces = [
        lax.dynamic_slice_in_dim(rows, (2 * pair + bit) * width, width, 1)
        for pair in range(rows.shape[1] // (2 * width))
    ]
    return pieces[0] if len(pieces) == 1 else jnp.concatenate(pieces, axis=1)


def ordered(upper_half, own_rows, partner_rows):
    lower_part = jnp.where(upper_half, partner_rows, own_rows)
    upper_part = jnp.where(upper_half, own_rows, partner_rows)
    return jnp.concatenate([lower_part, upper_part], axis=0)


def shards(snapshots, prior_basis, mass_factor, neighbours):
    weighted, gram = weigh(prior_basis, snapshots, mass_factor, neighbours)
    members = lax.axis_size("tm")
    places = members * lax.axis_size("space")
    across = [1 << i for i in range(members.bit_length() - 1, places.bit_length() - 1)]
    member = lax.axis_index("tm")
    width = snapshots.shape[1] // members
    partner_weighted = None
    reduced = (jax.ShapeDtypeStruct((RANK, 2 * RANK), BF16), jax.ShapeDtypeStruct((RANK, RANK), F32))
    coefficients, own = compress(first_kernel, reduced, total(gram, across, 2))
    for level in range(members.bit_length() - 1):
        step = 1 << level
        bit = member // step % 2
        upper_half = bit == 1
        if partner_weighted is None:
            weighted = combine(coefficients, weighted)
            partner_weighted = swapped(shared_out(weighted, width, 1 - bit), step)
            own_weighted = shared_out(weighted, width, bit)
        else:
            partner_weighted = combine(swapped(coefficients, step), partner_weighted)
            own_weighted = combine(coefficients, shared_out(weighted, width, bit))
        weighted = ordered(upper_half, own_weighted, partner_weighted)
        top = lax.dot_general(weighted[:RANK], weighted, NT, preferred_element_type=F32)
        last = 2 * step == members
        if not last:
            next_bit = member // (2 * step) % 2
            partner_weighted = swapped(shared_out(weighted, width, 1 - next_bit), 2 * step)
        bits = [1 << i for i in range(level + 1)] + across
        top = total(top, bits[:2], 2)
        coefficients, own, top = lax.optimization_barrier((coefficients, own, top))
        partner_own = swapped(own, step)
        if level == 0:
            stacked = combine_two(coefficients, prior_basis, snapshots)
        else:
            stacked = combine(coefficients, stacked)
        partner_stacked = swapped(shared_out(stacked, width, 1 - bit), step)
        stacked = ordered(upper_half, shared_out(stacked, width, bit), partner_stacked)
        top = total(top, bits[2:], 2)
        upper = jnp.where(upper_half, own, partner_own)
        if not last:
            coefficients, own = compress(merge_kernel, reduced, top, upper)
    share = jax.ShapeDtypeStruct((RANK, width), BF16)
    return compress(last_kernel, (share, share), top, upper, stacked, weighted)


def solution(mesh):
    return jax.shard_map(
        shards,
        mesh=mesh,
        in_specs=(P("tm", "space"), P("tm", "space"), P(None, None, "space"), P("space", None)),
        out_specs=(P(None, ("space", "tm")), P(None, ("space", "tm"))),
        check_vma=False,
    )
```
